768 devices in a mesh: ctx: 12 (over z), head: 64 (over x, y, core).
Axes of the slice: x: 4, y: 8, z: 12, core: 2. Of those that a mesh axis runs over, the one named last changes fastest.
Arguments:
- query_rows: bfloat16 [3072, 16384], P('ctx', 'head'), may hold values from -5 to 5
- key_rows: bfloat16 [3072, 1024], P('ctx'), may hold values from -5 to 5
- value_rows: bfloat16 [3072, 1024], P('ctx'), may hold values from -6 to 6
- out_grad: bfloat16 [3072, 16384], P('ctx', 'head'), may hold values from -16 to 16
- span_order: int32 [24], replicated, may hold values from 0 to 23, as said below
Outputs:
- attn_out: bfloat16 [3072, 16384], P('ctx', 'head')
- query_grad: bfloat16 [3072, 16384], P('ctx', 'head')
- key_grad: bfloat16 [3072, 1024], P(('ctx', 'head'))
- value_grad: bfloat16 [3072, 1024], P(('ctx', 'head'))
The draws below stay inside these ranges and needn't reach their ends.
Inputs may be any that keep to these rules, and one draw needn't show every extreme that they name: `span_order`: each of 0 to 23 appears once, and entries 2d and 2d + 1 add up to 23.
All inputs are finite; a program needn't handle non-finite values.
Results may differ from the reference program's by a relative error of at most 0.025.
Values may be sent and summed in bfloat16 or wider, within the bound.
A program may use at most 32 MiB of HBM per device.

```python
import math
import jax
import jax.numpy as jnp
from jax import lax

QUERY_HEADS = 128
KV_HEADS = 8
HEAD_DIM = 128
SPAN = 128
SPANS = 24
SEQ = 3072
GROUP = 16


def draw_query_rows(key, part):
    noise_key = jax.random.fold_in(key, 11)
    shaped = (SEQ, QUERY_HEADS * HEAD_DIM)
    entries = jnp.clip(jax.random.normal(noise_key, shaped, jnp.float32), -4.5, 4.5)
    return entries.astype(jnp.bfloat16)


def draw_key_rows(key, part):
    noise_key = jax.random.fold_in(key, 13)
    shaped = (SEQ, KV_HEADS * HEAD_DIM)
    entries = jnp.clip(jax.random.normal(noise_key, shaped, jnp.float32), -4.5, 4.5)
    return entries.astype(jnp.bfloat16)


def draw_span_order(key, part):
    pair_key, flip_key = jax.random.split(jax.random.fold_in(key, 17))
    halves = SPANS // 2
    pairs = jax.random.permutation(pair_key, halves).astype(jnp.int32)
    flips = jax.random.randint(flip_key, (halves,), 0, 2)
    first_span = jnp.where(flips == 1, pairs, SPANS - 1 - pairs)
    second_span = SPANS - 1 - first_span
    return jnp.stack([first_span, second_span], axis=1).reshape(SPANS).astype(jnp.int32)


def level_of(rng, dims, cuts, least, largest):
    factor_of, own = 1.0, jax.random.fold_in(rng, 6)
    for position, parts in cuts:
        heights = jnp.exp(jax.random.uniform(jax.random.fold_in(own, position), (parts,), jnp.float32, least / len(cuts), largest / len(cuts)))
        factor_of = factor_of * jnp.repeat(heights, dims[position] // parts).reshape([-1 if axis == position else 1 for axis in range(len(dims))])
    return factor_of


def gaussian(stream_key, shape, scale, bound, shards=(), held_as=jnp.bfloat16):
    loudness = level_of(stream_key, shape, shards, -0.22, 0.18) if shards else 1.0
    values = jax.random.normal(stream_key, shape, jnp.float32) * scale * loudness
    return jnp.minimum(jnp.maximum(values, -bound), bound).astype(held_as)


def setup_inputs(seed: int = 0) -> dict:
    keys = jax.random.split(jax.random.key(seed), 6)
    query_rows = draw_query_rows(jax.random.fold_in(keys[5], 71), 0)
    key_rows = draw_key_rows(jax.random.fold_in(keys[5], 71), 0)
    value_rows = gaussian(keys[2], (SEQ, KV_HEADS * HEAD_DIM), 1.0, 6.0, ((0, 12),))
    out_grad = gaussian(keys[3], (SEQ, QUERY_HEADS * HEAD_DIM), 4.0, 16.0, ((0, 12), (1, 64)))
    span_order = draw_span_order(jax.random.fold_in(keys[5], 71), 0)
    return dict(query_rows=query_rows, key_rows=key_rows, value_rows=value_rows, out_grad=out_grad, span_order=span_order)


def reference(query_rows, key_rows, value_rows, out_grad, span_order):
    score_scale = 1.0 / math.sqrt(HEAD_DIM)
    positions = (span_order[:, None] * SPAN + jnp.arange(SPAN, dtype=jnp.int32)[None, :]).reshape(SEQ)
    visible = positions[None, :] <= positions[:, None]
    query_heads = query_rows.reshape(SEQ, QUERY_HEADS, HEAD_DIM).transpose(1, 0, 2)
    grad_heads = out_grad.reshape(SEQ, QUERY_HEADS, HEAD_DIM).transpose(1, 0, 2)
    key_heads = key_rows.reshape(SEQ, KV_HEADS, HEAD_DIM).transpose(1, 0, 2)
    value_heads = value_rows.reshape(SEQ, KV_HEADS, HEAD_DIM).transpose(1, 0, 2)

    def attend_head(head_id):
        kv_group = head_id // GROUP
        query_head = query_heads[head_id]
        grad_head = grad_heads[head_id]
        key_head = key_heads[kv_group]
        value_head = value_heads[kv_group]
        scores = jnp.dot(query_head, key_head.T, preferred_element_type=jnp.float32) * score_scale
        scores = jnp.where(visible, scores, -jnp.inf)
        row_top = lax.optimization_barrier(jnp.max(scores, axis=1, keepdims=True))
        log_total = row_top + jnp.log(lax.optimization_barrier(jnp.sum(jnp.exp(scores - row_top), axis=1, keepdims=True)))
        probs = jnp.exp(scores - log_total)
        probs_low = probs.astype(jnp.bfloat16)
        attended = jnp.dot(probs_low, value_head, preferred_element_type=jnp.float32).astype(jnp.bfloat16)
        row_dots = lax.optimization_barrier(jnp.sum(grad_head.astype(jnp.float32) * attended.astype(jnp.float32), axis=1, keepdims=True))
        prob_grad = jnp.dot(grad_head, value_head.T, preferred_element_type=jnp.float32)
        score_grad = (probs * (prob_grad - row_dots)).astype(jnp.bfloat16)
        query_grads = (jnp.dot(score_grad, key_head, preferred_element_type=jnp.float32) * score_scale).astype(jnp.bfloat16)
        key_part = jnp.dot(score_grad.T, query_head, preferred_element_type=jnp.float32) * score_scale
        value_part = jnp.dot(probs_low.T, grad_head, preferred_element_type=jnp.float32)
        return (attended, query_grads, key_part, value_part)
    attended, query_grads, key_parts, value_parts = lax.map(attend_head, jnp.arange(QUERY_HEADS, dtype=jnp.int32))
    attn_out = attended.transpose(1, 0, 2).reshape(SEQ, QUERY_HEADS * HEAD_DIM)
    query_grad = query_grads.transpose(1, 0, 2).reshape(SEQ, QUERY_HEADS * HEAD_DIM)
    key_sums = key_parts.reshape(KV_HEADS, GROUP, SEQ, HEAD_DIM).sum(axis=1)
    value_sums = value_parts.reshape(KV_HEADS, GROUP, SEQ, HEAD_DIM).sum(axis=1)
    key_grad = key_sums.transpose(1, 0, 2).reshape(SEQ, KV_HEADS * HEAD_DIM).astype(jnp.bfloat16)
    value_grad = value_sums.transpose(1, 0, 2).reshape(SEQ, KV_HEADS * HEAD_DIM).astype(jnp.bfloat16)
    return (attn_out, query_grad, key_grad, value_grad)
```

```python
import functools
import math

import jax
import jax.numpy as jnp
from jax import lax
from jax.experimental import pallas as pl
from jax.experimental.pallas import tpu as pltpu
from jax.sharding import PartitionSpec as P

KV_HEADS = 8
HEAD_DIM = 128
SPAN = 128
HIDDEN = -1e30
F32 = jnp.float32
BF16 = jnp.bfloat16
MESH = pl.DeviceIdType.MESH
PLUS, MINUS = 0, 1
KEY, VAL = 0, 1


def dot(a, b):
    return jnp.dot(a, b, preferred_element_type=F32)


def attention_kernel(
    n_ctx,
    order_ref,
    q_hbm,
    k_hbm,
    v_hbm,
    g_hbm,
    o_ref,
    dq_ref,
    dk_ref,
    dv_ref,
    q4,
    g4,
    q_t,
    g_t,
    kv,
    kv_t,
    p_buf,
    dp_buf,
    m_blk,
    stat,
    stat_in,
    pb,
    dsb,
    o_t,
    dq_t,
    o_in,
    dq_in,
    rs_in,
    rs_out,
    y_out,
    y_in,
    f_out,
    f_in,
    load_sem,
    swap_send,
    swap_recv,
    kv_send,
    kv_recv,
    rs_send,
    rs_recv,
    y_send,
    y_recv,
    f_send,
    f_recv,
):
    half = n_ctx // 2
    z = lax.axis_index("ctx")
    head = lax.axis_index("head")
    group = head // 8
    quarter = (head % 8) // 2
    core = head % 2
    sibling = head + 1 - 2 * core
    after = lax.rem(z + 1, n_ctx)
    before = lax.rem(z + n_ctx - 1, n_ctx)
    score_scale = 1.0 / math.sqrt(HEAD_DIM)
    exponent_scale = score_scale * math.log2(math.e)

    rows = pl.ds(pl.multiple_of(core * SPAN, SPAN), SPAN)
    cols = pl.ds(pl.multiple_of(group * HEAD_DIM, HEAD_DIM), HEAD_DIM)
    loads = [
        pltpu.make_async_copy(k_hbm.at[rows, cols], kv.at[KEY, 0, pl.ds(0, SPAN)], load_sem.at[0]),
        pltpu.make_async_copy(v_hbm.at[rows, cols], kv.at[VAL, 0, pl.ds(0, SPAN)], load_sem.at[1]),
    ]
    for h in range(2):
        part = pl.ds(h * HEAD_DIM, HEAD_DIM)
        loads.append(pltpu.make_async_copy(q_hbm.at[:, part], q4.at[0, pl.ds(h * 256, 256)], load_sem.at[2 + h]))
        loads.append(pltpu.make_async_copy(g_hbm.at[:, part], g4.at[0, pl.ds(h * 256, 256)], load_sem.at[4 + h]))
    for load in loads:
        load.start()

    barrier = pltpu.get_barrier_semaphore()

    def greet(ctx_id, head_id):
        pl.semaphore_signal(barrier, inc=1, device_id=(ctx_id, head_id), device_id_type=MESH)

    greet(after, head)
    greet(before, head)
    greet(z, sibling)
    for step in range(1, 4):
        greet(z, group * 8 + 2 * lax.rem(quarter + step, 4) + core)
    span_of_rows = head // 32
    part_of_rows = lax.rem(head, 32) // 8
    own_chunk = group == core * 4 + quarter
    for g in range(KV_HEADS):

        @pl.when(jnp.logical_not(jnp.logical_and(own_chunk, group == g)))
        def _():
            greet(z, g * 8 + 2 * part_of_rows + span_of_rows)

    def remote(src, dst, send, recv, ctx_id, head_id):
        return pltpu.make_async_remote_copy(
            src_ref=src,
            dst_ref=dst,
            send_sem=send,
            recv_sem=recv,
            device_id=(ctx_id, head_id),
            device_id_type=MESH,
        )

    def slot(kind, t, side):
        return kv.at[kind, t, pl.ds(side * SPAN, SPAN)]

    def hop(kind, direction, t, last=False):
        if direction == PLUS:
            src = slot(kind, t - 1, 0)
            dst = slot(kind, 0, 1) if last else slot(kind, t, 0)
            to = after
        else:
            src = slot(kind, t - 1, 1)
            if isinstance(t, int) and t == 1:
                src = slot(kind, 0, 0)
            dst = slot(kind, 0, 1) if last else slot(kind, t, 1)
            to = before
        return remote(src, dst, kv_send.at[direction, kind, t - 1], kv_recv.at[direction, kind, t - 1], to, head)

    for load in loads[:2]:
        load.wait()
    self_targets = jnp.where(own_chunk, 1, 0)
    pl.semaphore_wait(barrier, 6 + KV_HEADS - self_targets)
    for kind in (KEY, VAL):
        for direction in (PLUS, MINUS):
            hop(kind, direction, 1).start()
    for load in loads[2:]:
        load.wait()
    swap_q = remote(q4.at[0], q4.at[1], swap_send.at[0], swap_recv.at[0], z, sibling)
    swap_g = remote(g4.at[0], g4.at[1], swap_send.at[1], swap_recv.at[1], z, sibling)
    swap_q.start()
    swap_g.start()

    stat[0:1, :] = jnp.full((1, 1024), HIDDEN, F32)
    stat[1:8, :] = jnp.zeros((7, 1024), F32)
    o_t[...] = jnp.zeros_like(o_t)
    dq_t[...] = jnp.zeros_like(dq_t)
    rs_in[PLUS, VAL, half - 1] = jnp.zeros((SPAN, HEAD_DIM), BF16)
    rs_in[MINUS, KEY, half - 1] = jnp.zeros((SPAN, HEAD_DIM), BF16)

    def turn(side):
        for h in range(2):
            q_t[:, side * 512 + h * 256 : side * 512 + (h + 1) * 256] = q4[side, h * 256 : (h + 1) * 256, :].T
            g_t[:, side * 512 + h * 256 : side * 512 + (h + 1) * 256] = g4[side, h * 256 : (h + 1) * 256, :].T

    turn(0)
    swap_q.wait_recv()
    swap_g.wait_recv()
    turn(1)

    lane = lax.broadcasted_iota(jnp.int32, (1, 256), 1)
    ahead = lax.broadcasted_iota(jnp.int32, (SPAN, 256), 0) - lax.rem(
        lax.broadcasted_iota(jnp.int32, (SPAN, 256), 1), SPAN
    )
    q_span0 = order_ref[2 * z]
    q_span1 = order_ref[2 * z + 1]

    def forward(t, side, block):
        k_span = order_ref[2 * block + core]
        reach = jnp.where(lane < SPAN, (q_span0 - k_span) * SPAN, (q_span1 - k_span) * SPAN)
        visible = ahead <= reach
        part = pl.ds(side * SPAN, SPAN)
        key = kv[KEY, t, part]
        value = kv[VAL, t, part]
        for h in range(4):
            at = slice(h * 256, (h + 1) * 256)
            s = jnp.where(visible, dot(key, q_t[:, at]) * exponent_scale, HIDDEN)
            top = stat[0:1, at]
            new_top = jnp.maximum(top, jnp.max(s, axis=0, keepdims=True))
            p = jnp.exp2(s - new_top)
            dp = dot(value, g_t[:, at])
            shrink = jnp.exp2(top - new_top)
            stat[1:2, at] = stat[1:2, at] * shrink + jnp.sum(p, axis=0, keepdims=True)
            stat[2:3, at] = stat[2:3, at] * shrink + jnp.sum(p * dp, axis=0, keepdims=True)
            stat[0:1, at] = new_top
            m_blk[t, side, 0:1, at] = new_top
            p_buf[t, part, at] = p
            dp_buf[t, part, at] = dp
        kv_t[KEY, t, :, part] = key.T
        kv_t[VAL, t, :, part] = value.T

    forward(0, 0, z)

    def gather_step(t, carry):
        for kind in (KEY, VAL):
            for direction in (PLUS, MINUS):
                hop(kind, direction, t).wait_recv()

                @pl.when(t < half - 1)
                def _():
                    hop(kind, direction, t + 1).start()

                if (kind == KEY) == (direction == PLUS):

                    @pl.when(t == half - 1)
                    def _():
                        hop(kind, direction, t + 1, last=True).start()

        forward(t, 0, lax.rem(z - t + n_ctx, n_ctx))
        forward(t, 1, lax.rem(z + t, n_ctx))
        return carry

    lax.fori_loop(1, half, gather_step, 0)
    hop(KEY, PLUS, half, last=True).wait_recv()
    hop(VAL, MINUS, half, last=True).wait_recv()
    forward(0, 1, lax.rem(z + half, n_ctx))

    swap_stat = remote(stat, stat_in, swap_send.at[2], swap_recv.at[2], z, sibling)
    swap_stat.start()
    swap_stat.wait()
    for mine in range(2):
        at = slice(mine * 512, (mine + 1) * 512)
        other = slice((1 - mine) * 512, (2 - mine) * 512)
        m_own, l_own, d_own = stat[0:1, at], stat[1:2, at], stat[2:3, at]
        m_sib, l_sib, d_sib = stat_in[0:1, other], stat_in[1:2, other], stat_in[2:3, other]
        top = jnp.maximum(m_own, m_sib)
        w_own, w_sib = jnp.exp2(m_own - top), jnp.exp2(m_sib - top)
        inverse = 1.0 / (l_own * w_own + l_sib * w_sib)
        stat[3:4, at] = top
        stat[4:5, at] = inverse
        stat[5:6, at] = (d_own * w_own + d_sib * w_sib) * inverse

    def probs_of(t, sides):
        for side in sides:
            part = pl.ds(side * SPAN, SPAN)
            for h in range(4):
                at = slice(h * 256, (h + 1) * 256)
                factor = jnp.exp2(m_blk[t, side, 0:1, at] - stat[3:4, at]) * stat[4:5, at]
                p = p_buf[t, part, at] * factor
                pb[part, at] = p.astype(BF16)
                dsb[part, at] = (p * (dp_buf[t, part, at] - stat[5:6, at])).astype(BF16)

    def grads_of(sides):
        part = pl.ds(sides[0] * SPAN, len(sides) * SPAN)
        value_grad = dot(pb[part, 0:512], g4[0]) + dot(pb[part, 512:1024], g4[1])
        key_grad = (dot(dsb[part, 0:512], q4[0]) + dot(dsb[part, 512:1024], q4[1])) * score_scale
        return key_grad, value_grad

    def rows_add(t):
        for side in range(2):
            at = slice(side * 512, (side + 1) * 512)
            o_t[side] += dot(kv_t[VAL, t], pb[:, at])
            dq_t[side] += dot(kv_t[KEY, t], dsb[:, at])

    def pass_on(kind, direction, d):
        return remote(
            rs_out.at[direction, kind, d - 1],
            rs_in.at[direction, kind, d - 1],
            rs_send.at[direction, kind, d - 1],
            rs_recv.at[direction, kind, d - 1],
            after if direction == PLUS else before,
            head,
        )

    probs_of(0, (0, 1))
    key_grad, value_grad = grads_of((0, 1))
    rs_out[PLUS, KEY, half - 1] = key_grad[SPAN:].astype(BF16)
    pass_on(KEY, PLUS, half).start()
    rs_out[MINUS, VAL, half - 1] = value_grad[SPAN:].astype(BF16)
    pass_on(VAL, MINUS, half).start()
    own_key_grad = key_grad[:SPAN]
    own_value_grad = value_grad[:SPAN]
    o_in[0] = own_key_grad
    o_in[1] = own_value_grad
    rows_add(0)

    def reduce_step(i, carry):
        d = half - 1 - i
        probs_of(d, (0, 1))
        key_grad, value_grad = grads_of((0, 1))
        for kind, grad in ((KEY, key_grad), (VAL, value_grad)):
            for direction in (PLUS, MINUS):
                mine = grad[SPAN:] if direction == PLUS else grad[:SPAN]
                if (kind == KEY) == (direction == PLUS):
                    pass_on(kind, direction, d + 1).wait_recv()
                else:

                    @pl.when(d < half - 1)
                    def _():
                        pass_on(kind, direction, d + 1).wait_recv()

                rs_out[direction, kind, d - 1] = (mine + rs_in[direction, kind, d].astype(F32)).astype(BF16)
                pass_on(kind, direction, d).start()
        rows_add(d)
        return carry

    lax.fori_loop(0, half - 1, reduce_step, 0)

    swap_o = remote(o_t.at[1], dq_in.at[0], swap_send.at[3], swap_recv.at[3], z, sibling)
    swap_dq = remote(dq_t.at[1], dq_in.at[1], swap_send.at[4], swap_recv.at[4], z, sibling)
    swap_o.start()
    swap_dq.start()

    for kind in (KEY, VAL):
        for direction in (PLUS, MINUS):
            pass_on(kind, direction, 1).wait_recv()
        total = o_in[kind] + rs_in[PLUS, kind, 0].astype(F32) + rs_in[MINUS, kind, 0].astype(F32)
        o_in[kind] = total
        for q in range(4):
            y_out[q, kind * 32 : (kind + 1) * 32, :] = total[q * 32 : (q + 1) * 32].astype(BF16)

    def to_quarter(step):
        other = lax.rem(quarter + step, 4)
        return remote(
            y_out.at[other], y_in.at[step - 1], y_send.at[step - 1], y_recv.at[step - 1], z, group * 8 + 2 * other + core
        )

    for step in range(1, 4):
        to_quarter(step).start()

    swap_o.wait_recv()
    swap_dq.wait_recv()
    for h in range(2):
        at = slice(h * 256, (h + 1) * 256)
        o_ref[:, h * HEAD_DIM : (h + 1) * HEAD_DIM] = (o_t[0, :, at] + dq_in[0, :, at]).T.astype(BF16)
        dq_ref[:, h * HEAD_DIM : (h + 1) * HEAD_DIM] = ((dq_t[0, :, at] + dq_in[1, :, at]) * score_scale).T.astype(BF16)

    chunk = pl.ds(pl.multiple_of(quarter * 32, 32), 32)
    sums = [o_in[kind, chunk, :] for kind in (KEY, VAL)]
    for step in range(1, 4):
        to_quarter(step).wait_recv()
        sums = [sums[kind] + y_in[step - 1, kind * 32 : (kind + 1) * 32, :].astype(F32) for kind in (KEY, VAL)]
    for n in range(8):
        f_out[n, 0:4, :] = sums[KEY][4 * n : 4 * n + 4]
        f_out[n, 4:8, :] = sums[VAL][4 * n : 4 * n + 4]

    def to_owner(n):
        return remote(f_out.at[n], f_in.at[group], f_send.at[n], f_recv.at[0], z, core * 32 + quarter * 8 + n)

    def to_self(n):
        return pltpu.make_async_copy(f_out.at[n], f_in.at[group], f_recv.at[0])

    for n in range(8):
        here = head == core * 32 + quarter * 8 + n

        @pl.when(here)
        def _():
            to_self(n).start()

        @pl.when(jnp.logical_not(here))
        def _():
            to_owner(n).start()

    swap_q.wait_send()
    swap_g.wait_send()
    swap_o.wait_send()
    swap_dq.wait_send()

    def sent(t, carry):
        for kind in (KEY, VAL):
            for direction in (PLUS, MINUS):
                hop(kind, direction, t).wait_send()
                pass_on(kind, direction, t).wait_send()
        return carry

    lax.fori_loop(1, half, sent, 0)
    hop(KEY, PLUS, half, last=True).wait_send()
    hop(VAL, MINUS, half, last=True).wait_send()
    pass_on(KEY, PLUS, half).wait_send()
    pass_on(VAL, MINUS, half).wait_send()
    for step in range(1, 4):
        to_quarter(step).wait_send()
    for n in range(8):

        @pl.when(jnp.logical_not(head == core * 32 + quarter * 8 + n))
        def _():
            to_owner(n).wait_send()

    pltpu.make_async_copy(f_out, f_in, f_recv.at[0]).wait()
    for g in range(KV_HEADS):
        at = slice(g * HEAD_DIM, (g + 1) * HEAD_DIM)
        dk_ref[:, at] = f_in[g, 0:4, :].astype(BF16)
        dv_ref[:, at] = f_in[g, 4:8, :].astype(BF16)


def per_device(query_rows, key_rows, value_rows, out_grad, span_order):
    n_ctx = lax.axis_size("ctx")
    half = n_ctx // 2
    vmem = pltpu.VMEM
    dma = pltpu.SemaphoreType.DMA
    anywhere = pl.BlockSpec(memory_space=pl.ANY)
    local = pl.BlockSpec(memory_space=pltpu.VMEM)
    return pl.pallas_call(
        functools.partial(attention_kernel, n_ctx),
        out_shape=(
            jax.ShapeDtypeStruct((256, 256), BF16),
            jax.ShapeDtypeStruct((256, 256), BF16),
            jax.ShapeDtypeStruct((4, 1024), BF16),
            jax.ShapeDtypeStruct((4, 1024), BF16),
        ),
        in_specs=[pl.BlockSpec(memory_space=pltpu.SMEM), anywhere, anywhere, anywhere, anywhere],
        out_specs=(local, local, local, local),
        scratch_shapes=[
            vmem((2, 512, 128), BF16),
            vmem((2, 512, 128), BF16),
            vmem((128, 1024), BF16),
            vmem((128, 1024), BF16),
            vmem((2, half, 256, 128), BF16),
            vmem((2, half, 128, 256), BF16),
            vmem((half, 256, 1024), F32),
            vmem((half, 256, 1024), F32),
            vmem((half, 2, 8, 1024), F32),
            vmem((8, 1024), F32),
            vmem((8, 1024), F32),
            vmem((256, 1024), BF16),
            vmem((256, 1024), BF16),
            vmem((2, 128, 512), F32),
            vmem((2, 128, 512), F32),
            vmem((2, 128, 128), F32),
            vmem((2, 128, 512), F32),
            vmem((2, 2, half, 128, 128), BF16),
            vmem((2, 2, half, 128, 128), BF16),
            vmem((4, 64, 128), BF16),
            vmem((3, 64, 128), BF16),
            vmem((8, 8, 128), F32),
            vmem((8, 8, 128), F32),
            dma((6,)),
            dma((5,)),
            dma((5,)),
            dma((2, 2, half)),
            dma((2, 2, half)),
            dma((2, 2, half)),
            dma((2, 2, half)),
            dma((3,)),
            dma((3,)),
            dma((8,)),
            dma((1,)),
        ],
        compiler_params=pltpu.CompilerParams(
            collective_id=0, has_side_effects=True, vmem_limit_bytes=48 * 1024 * 1024
        ),
    )(span_order, query_rows, key_rows, value_rows, out_grad)


def solution(mesh):
    in_specs = (P("ctx", "head"), P("ctx", None), P("ctx", None), P("ctx", "head"), P())
    out_specs = (
        P("ctx", "head"),
        P("ctx", "head"),
        P(("ctx", "head"), None),
        P(("ctx", "head"), None),
    )
    return jax.shard_map(
        per_device, mesh=mesh, in_specs=in_specs, out_specs=out_specs, check_vma=False
    )
```

```python
import functools
import math

import jax
import jax.numpy as jnp
from jax import lax
from jax.experimental import pallas as pl
from jax.experimental.pallas import tpu as pltpu
from jax.sharding import PartitionSpec as P

KV_HEADS = 8
HEAD_DIM = 128
SPAN = 128
HIDDEN = -1e30
F32 = jnp.float32
BF16 = jnp.bfloat16
MESH = pl.DeviceIdType.MESH
PLUS, MINUS = 0, 1
KEY, VAL = 0, 1


def dot(a, b):
    return jnp.dot(a, b, preferred_element_type=F32)


def attention_kernel(
    n_ctx,
    order_ref,
    q_hbm,
    k_hbm,
    v_hbm,
    g_hbm,
    o_ref,
    dq_ref,
    dk_ref,
    dv_ref,
    q4,
    g4,
    q_t,
    g_t,
    kv,
    kv_t,
    p_buf,
    dp_buf,
    m_blk,
    stat,
    stat_in,
    pb,
    dsb,
    o_t,
    dq_t,
    o_in,
    dq_in,
    rs_in,
    rs_out,
    y_out,
    y_in,
    f_out,
    f_in,
    load_sem,
    swap_send,
    swap_recv,
    kv_send,
    kv_recv,
    rs_send,
    rs_recv,
    y_send,
    y_recv,
    f_send,
    f_recv,
):
    half = n_ctx // 2
    z = lax.axis_index("ctx")
    head = lax.axis_index("head")
    group = head // 8
    quarter = (head % 8) // 2
    core = head % 2
    sibling = head + 1 - 2 * core

    def along(direction, reach):
        return lax.rem(z + (reach if direction == PLUS else n_ctx - reach), n_ctx)

    score_scale = 1.0 / math.sqrt(HEAD_DIM)
    exponent_scale = score_scale * math.log2(math.e)

    rows = pl.ds(pl.multiple_of(core * SPAN, SPAN), SPAN)
    cols = pl.ds(pl.multiple_of(group * HEAD_DIM, HEAD_DIM), HEAD_DIM)
    loads = [
        pltpu.make_async_copy(k_hbm.at[rows, cols], kv.at[0, 0, KEY], load_sem.at[0]),
        pltpu.make_async_copy(v_hbm.at[rows, cols], kv.at[0, 0, VAL], load_sem.at[1]),
    ]
    for h in range(2):
        part = pl.ds(h * HEAD_DIM, HEAD_DIM)
        loads.append(pltpu.make_async_copy(q_hbm.at[:, part], q4.at[0, pl.ds(h * 256, 256)], load_sem.at[2 + h]))
        loads.append(pltpu.make_async_copy(g_hbm.at[:, part], g4.at[0, pl.ds(h * 256, 256)], load_sem.at[4 + h]))
    for load in loads:
        load.start()

    barrier = pltpu.get_barrier_semaphore()

    def greet(ctx_id, head_id):
        pl.semaphore_signal(barrier, inc=1, device_id=(ctx_id, head_id), device_id_type=MESH)

    for direction in (PLUS, MINUS):
        for reach in (1, 2):
            greet(along(direction, reach), head)
    greet(z, sibling)
    for step in range(1, 4):
        greet(z, group * 8 + 2 * lax.rem(quarter + step, 4) + core)
    span_of_rows = head // 32
    part_of_rows = lax.rem(head, 32) // 8
    own_chunk = group == core * 4 + quarter
    for g in range(KV_HEADS):

        @pl.when(jnp.logical_not(jnp.logical_and(own_chunk, group == g)))
        def _():
            greet(z, g * 8 + 2 * part_of_rows + span_of_rows)

    def remote(src, dst, send, recv, ctx_id, head_id):
        return pltpu.make_async_remote_copy(
            src_ref=src,
            dst_ref=dst,
            send_sem=send,
            recv_sem=recv,
            device_id=(ctx_id, head_id),
            device_id_type=MESH,
        )

    def hop(direction, source, reach):
        t = source + reach
        src = kv.at[source, direction if source else 0]
        dst = kv.at[t % half, direction if t < half else 1]
        if t == half:
            kind = KEY if direction == PLUS else VAL
            src, dst = src.at[kind], dst.at[kind]
        return remote(src, dst, kv_send.at[direction, t - 1], kv_recv.at[direction, t - 1], along(direction, reach), head)

    def hops(source, action):
        for reach in (2, 1):
            for direction in (PLUS, MINUS):
                getattr(hop(direction, source, reach), action)()

    def arrived(t):
        for direction in (PLUS, MINUS):
            hop(direction, (t - 1) // 2 * 2, 1 + (t - 1) % 2).wait_recv()

    for load in loads[:2]:
        load.wait()
    self_targets = jnp.where(own_chunk, 1, 0)
    pl.semaphore_wait(barrier, 8 + KV_HEADS - self_targets)
    hops(0, "start")
    for load in loads[2:]:
        load.wait()
    swap_q = remote(q4.at[0], q4.at[1], swap_send.at[0], swap_recv.at[0], z, sibling)
    swap_g = remote(g4.at[0], g4.at[1], swap_send.at[1], swap_recv.at[1], z, sibling)
    swap_q.start()
    swap_g.start()

    stat[0:1, :] = jnp.full((1, 1024), HIDDEN, F32)
    stat[1:8, :] = jnp.zeros((7, 1024), F32)
    o_t[...] = jnp.zeros_like(o_t)
    dq_t[...] = jnp.zeros_like(dq_t)
    rs_in[PLUS, half - 1, VAL] = jnp.zeros((SPAN, HEAD_DIM), BF16)
    rs_in[MINUS, half - 1, KEY] = jnp.zeros((SPAN, HEAD_DIM), BF16)

    def turn(side):
        for h in range(2):
            q_t[:, side * 512 + h * 256 : side * 512 + (h + 1) * 256] = q4[side, h * 256 : (h + 1) * 256, :].T
            g_t[:, side * 512 + h * 256 : side * 512 + (h + 1) * 256] = g4[side, h * 256 : (h + 1) * 256, :].T

    turn(0)
    swap_q.wait_recv()
    swap_g.wait_recv()
    turn(1)

    lane = lax.broadcasted_iota(jnp.int32, (1, 256), 1)
    ahead = lax.broadcasted_iota(jnp.int32, (SPAN, 256), 0) - lax.rem(
        lax.broadcasted_iota(jnp.int32, (SPAN, 256), 1), SPAN
    )
    q_span0 = order_ref[2 * z]
    q_span1 = order_ref[2 * z + 1]

    def forward(t, side, block):
        k_span = order_ref[2 * block + core]
        reach = jnp.where(lane < SPAN, (q_span0 - k_span) * SPAN, (q_span1 - k_span) * SPAN)
        visible = ahead <= reach
        part = pl.ds(side * SPAN, SPAN)
        key = kv[t, side, KEY]
        value = kv[t, side, VAL]
        for h in range(4):
            at = slice(h * 256, (h + 1) * 256)
            s = jnp.where(visible, dot(key, q_t[:, at]) * exponent_scale, HIDDEN)
            top = stat[0:1, at]
            new_top = jnp.maximum(top, jnp.max(s, axis=0, keepdims=True))
            p = jnp.exp2(s - new_top)
            dp = dot(value, g_t[:, at])
            shrink = jnp.exp2(top - new_top)
            stat[1:2, at] = stat[1:2, at] * shrink + jnp.sum(p, axis=0, keepdims=True)
            stat[2:3, at] = stat[2:3, at] * shrink + jnp.sum(p * dp, axis=0, keepdims=True)
            stat[0:1, at] = new_top
            m_blk[t, side, 0:1, at] = new_top
            p_buf[t, part, at] = p
            dp_buf[t, part, at] = dp
        kv_t[KEY, t, :, part] = key.T
        kv_t[VAL, t, :, part] = value.T

    forward(0, 0, z)

    def gather_step(t, carry):
        for far in range(2, half, 2):

            @pl.when(t == far - 1)
            def _():
                arrived(far)
                hops(far, "start")
                arrived(far - 1)

        @pl.when(t == half - 1)
        def _():
            arrived(half - 1)

        forward(t, 0, lax.rem(z - t + n_ctx, n_ctx))
        forward(t, 1, lax.rem(z + t, n_ctx))
        return carry

    lax.fori_loop(1, half, gather_step, 0)
    arrived(half)
    forward(0, 1, lax.rem(z + half, n_ctx))

    swap_stat = remote(stat, stat_in, swap_send.at[2], swap_recv.at[2], z, sibling)
    swap_stat.start()
    swap_stat.wait()
    for mine in range(2):
        at = slice(mine * 512, (mine + 1) * 512)
        other = slice((1 - mine) * 512, (2 - mine) * 512)
        m_own, l_own, d_own = stat[0:1, at], stat[1:2, at], stat[2:3, at]
        m_sib, l_sib, d_sib = stat_in[0:1, other], stat_in[1:2, other], stat_in[2:3, other]
        top = jnp.maximum(m_own, m_sib)
        w_own, w_sib = jnp.exp2(m_own - top), jnp.exp2(m_sib - top)
        inverse = 1.0 / (l_own * w_own + l_sib * w_sib)
        stat[3:4, at] = top
        stat[4:5, at] = inverse
        stat[5:6, at] = (d_own * w_own + d_sib * w_sib) * inverse

    def probs_of(t, sides):
        for side in sides:
            part = pl.ds(side * SPAN, SPAN)
            for h in range(4):
                at = slice(h * 256, (h + 1) * 256)
                factor = jnp.exp2(m_blk[t, side, 0:1, at] - stat[3:4, at]) * stat[4:5, at]
                p = p_buf[t, part, at] * factor
                pb[part, at] = p.astype(BF16)
                dsb[part, at] = (p * (dp_buf[t, part, at] - stat[5:6, at])).astype(BF16)

    def grads_of(sides):
        part = pl.ds(sides[0] * SPAN, len(sides) * SPAN)
        value_grad = dot(pb[part, 0:512], g4[0]) + dot(pb[part, 512:1024], g4[1])
        key_grad = (dot(dsb[part, 0:512], q4[0]) + dot(dsb[part, 512:1024], q4[1])) * score_scale
        return key_grad, value_grad

    def rows_add(t):
        for side in range(2):
            at = slice(side * 512, (side + 1) * 512)
            o_t[side] += dot(kv_t[VAL, t], pb[:, at])
            dq_t[side] += dot(kv_t[KEY, t], dsb[:, at])

    def pass_on(direction, d):
        src, dst = rs_out.at[direction, d - 1], rs_in.at[direction, d - 1]
        if isinstance(d, int) and d == half:
            kind = KEY if direction == PLUS else VAL
            src, dst = src.at[kind], dst.at[kind]
        reach = 2 - d % 2
        return remote(src, dst, rs_send.at[direction, d - 1], rs_recv.at[direction, d - 1], along(direction, reach), head)

    probs_of(0, (0, 1))
    key_grad, value_grad = grads_of((0, 1))
    rs_out[PLUS, half - 1, KEY] = key_grad[SPAN:].astype(BF16)
    pass_on(PLUS, half).start()
    rs_out[MINUS, half - 1, VAL] = value_grad[SPAN:].astype(BF16)
    pass_on(MINUS, half).start()
    own_key_grad = key_grad[:SPAN]
    own_value_grad = value_grad[:SPAN]
    o_in[0] = own_key_grad
    o_in[1] = own_value_grad
    rows_add(0)

    def reduce_step(i, carry):
        d = half - 1 - 2 * ((i + 1) // 2) + (i + 1) % 2 - 1 // (i + 1)
        probs_of(d, (0, 1))
        grads = grads_of((0, 1))
        for direction in (PLUS, MINUS):
            part = slice(SPAN, 2 * SPAN) if direction == PLUS else slice(0, SPAN)

            @pl.when(d % 2 == 1)
            def _():
                for kind in (KEY, VAL):
                    rs_out[direction, d - 1, kind] = grads[kind][part].astype(BF16)

            @pl.when(d % 2 == 0)
            def _():
                pass_on(direction, d + 1).wait_recv()
                for far in range(2, half, 2):

                    @pl.when(d == far)
                    def _():
                        pass_on(direction, far + 2).wait_recv()

                for kind in (KEY, VAL):
                    beyond = rs_in[direction, d, kind].astype(F32) + rs_in[direction, d + 1, kind].astype(F32)
                    rs_out[direction, d - 1, kind] = (grads[kind][part] + beyond).astype(BF16)

            pass_on(direction, d).start()
        rows_add(d)
        return carry

    lax.fori_loop(0, half - 1, reduce_step, 0)

    swap_o = remote(o_t.at[1], dq_in.at[0], swap_send.at[3], swap_recv.at[3], z, sibling)
    swap_dq = remote(dq_t.at[1], dq_in.at[1], swap_send.at[4], swap_recv.at[4], z, sibling)
    swap_o.start()
    swap_dq.start()

    for direction in (PLUS, MINUS):
        for d in (1, 2):
            pass_on(direction, d).wait_recv()
    for kind in (KEY, VAL):
        total = o_in[kind]
        for direction in (PLUS, MINUS):
            for d in (1, 2):
                total += rs_in[direction, d - 1, kind].astype(F32)
        o_in[kind] = total
        for q in range(4):
            y_out[q, kind * 32 : (kind + 1) * 32, :] = total[q * 32 : (q + 1) * 32].astype(BF16)

    def to_quarter(step):
        other = lax.rem(quarter + step, 4)
        return remote(
            y_out.at[other], y_in.at[step - 1], y_send.at[step - 1], y_recv.at[step - 1], z, group * 8 + 2 * other + core
        )

    for step in range(1, 4):
        to_quarter(step).start()

    swap_o.wait_recv()
    swap_dq.wait_recv()
    for h in range(2):
        at = slice(h * 256, (h + 1) * 256)
        o_ref[:, h * HEAD_DIM : (h + 1) * HEAD_DIM] = (o_t[0, :, at] + dq_in[0, :, at]).T.astype(BF16)
        dq_ref[:, h * HEAD_DIM : (h + 1) * HEAD_DIM] = ((dq_t[0, :, at] + dq_in[1, :, at]) * score_scale).T.astype(BF16)

    chunk = pl.ds(pl.multiple_of(quarter * 32, 32), 32)
    sums = [o_in[kind, chunk, :] for kind in (KEY, VAL)]
    for step in range(1, 4):
        to_quarter(step).wait_recv()
        sums = [sums[kind] + y_in[step - 1, kind * 32 : (kind + 1) * 32, :].astype(F32) for kind in (KEY, VAL)]
    for n in range(8):
        f_out[n, 0:4, :] = sums[KEY][4 * n : 4 * n + 4]
        f_out[n, 4:8, :] = sums[VAL][4 * n : 4 * n + 4]

    def to_owner(n):
        return remote(f_out.at[n], f_in.at[group], f_send.at[n], f_recv.at[0], z, core * 32 + quarter * 8 + n)

    def to_self(n):
        return pltpu.make_async_copy(f_out.at[n], f_in.at[group], f_recv.at[0])

    for n in range(8):
        here = head == core * 32 + quarter * 8 + n

        @pl.when(here)
        def _():
            to_self(n).start()

        @pl.when(jnp.logical_not(here))
        def _():
            to_owner(n).start()

    swap_q.wait_send()
    swap_g.wait_send()
    swap_o.wait_send()
    swap_dq.wait_send()

    for source in range(0, half, 2):
        hops(source, "wait_send")
    for direction in (PLUS, MINUS):
        for d in range(1, half + 1):
            pass_on(direction, d).wait_send()
    for step in range(1, 4):
        to_quarter(step).wait_send()
    for n in range(8):

        @pl.when(jnp.logical_not(head == core * 32 + quarter * 8 + n))
        def _():
            to_owner(n).wait_send()

    pltpu.make_async_copy(f_out, f_in, f_recv.at[0]).wait()
    for g in range(KV_HEADS):
        at = slice(g * HEAD_DIM, (g + 1) * HEAD_DIM)
        dk_ref[:, at] = f_in[g, 0:4, :].astype(BF16)
        dv_ref[:, at] = f_in[g, 4:8, :].astype(BF16)


def per_device(query_rows, key_rows, value_rows, out_grad, span_order):
    n_ctx = lax.axis_size("ctx")
    half = n_ctx // 2
    vmem = pltpu.VMEM
    dma = pltpu.SemaphoreType.DMA
    anywhere = pl.BlockSpec(memory_space=pltpu.HBM)
    local = pl.BlockSpec(memory_space=pltpu.VMEM)
    return pl.pallas_call(
        functools.partial(attention_kernel, n_ctx),
        out_shape=(
            jax.ShapeDtypeStruct((256, 256), BF16),
            jax.ShapeDtypeStruct((256, 256), BF16),
            jax.ShapeDtypeStruct((4, 1024), BF16),
            jax.ShapeDtypeStruct((4, 1024), BF16),
        ),
        in_specs=[pl.BlockSpec(memory_space=pltpu.SMEM), anywhere, anywhere, anywhere, anywhere],
        out_specs=(local, local, local, local),
        scratch_shapes=[
            vmem((2, 512, 128), BF16),
            vmem((2, 512, 128), BF16),
            vmem((128, 1024), BF16),
            vmem((128, 1024), BF16),
            vmem((half, 2, 2, 128, 128), BF16),
            vmem((2, half, 128, 256), BF16),
            vmem((half, 256, 1024), F32),
            vmem((half, 256, 1024), F32),
            vmem((half, 2, 8, 1024), F32),
            vmem((8, 1024), F32),
            vmem((8, 1024), F32),
            vmem((256, 1024), BF16),
            vmem((256, 1024), BF16),
            vmem((2, 128, 512), F32),
            vmem((2, 128, 512), F32),
            vmem((2, 128, 128), F32),
            vmem((2, 128, 512), F32),
            vmem((2, half, 2, 128, 128), BF16),
            vmem((2, half, 2, 128, 128), BF16),
            vmem((4, 64, 128), BF16),
            vmem((3, 64, 128), BF16),
            vmem((8, 8, 128), F32),
            vmem((8, 8, 128), F32),
            dma((6,)),
            dma((5,)),
            dma((5,)),
            dma((2, half)),
            dma((2, half)),
            dma((2, half)),
            dma((2, half)),
            dma((3,)),
            dma((3,)),
            dma((8,)),
            dma((1,)),
        ],
        compiler_params=pltpu.CompilerParams(
            collective_id=0, has_side_effects=True, vmem_limit_bytes=62 * 1024 * 1024
        ),
    )(span_order, query_rows, key_rows, value_rows, out_grad)


def solution(mesh):
    in_specs = (P("ctx", "head"), P("ctx", None), P("ctx", None), P("ctx", "head"), P())
    out_specs = (
        P("ctx", "head"),
        P("ctx", "head"),
        P(("ctx", "head"), None),
        P(("ctx", "head"), None),
    )
    return jax.shard_map(
        per_device, mesh=mesh, in_specs=in_specs, out_specs=out_specs, check_vma=False
    )
```

```python
import functools
import math

import jax
import jax.numpy as jnp
from jax import lax
from jax.experimental import pallas as pl
from jax.experimental.pallas import tpu as pltpu
from jax.sharding import PartitionSpec as P

HEAD_DIM = 128
SPAN = 128
PIECE = 64
QUADS = 16
HIDDEN = -1e30
F32 = jnp.float32
BF16 = jnp.bfloat16
MESH = pl.DeviceIdType.MESH
PLUS, MINUS = 0, 1
KEY, VAL = 0, 1
SIB, PAIR, DIAG = 1, 2, 3
REACH = 3


def dot(a, b):
    return jnp.dot(a, b, preferred_element_type=F32)


def attention_kernel(
    n_ctx,
    order_ref,
    q_hbm,
    k_hbm,
    v_hbm,
    g_hbm,
    o_ref,
    dq_ref,
    dk_ref,
    dv_ref,
    q8,
    g8,
    q_t,
    g_t,
    kv,
    kv_t,
    p_buf,
    dp_buf,
    m_blk,
    stat,
    stat_in,
    both,
    pb,
    dsb,
    o_t,
    dq_t,
    mid_out,
    mid_in,
    last_out,
    last_in,
    own_grad,
    near_grad,
    rs_in,
    rs_out,
    f_out,
    f_in,
    load_sem,
    swap_send,
    swap_recv,
    kv_send,
    kv_recv,
    rs_send,
    rs_recv,
    f_send,
    f_recv,
):
    half = n_ctx // 2
    z = lax.axis_index("ctx")
    head = lax.axis_index("head")
    group = head // 8
    quad = head // 4
    member = head % 4
    core = head % 2
    chip = member // 2
    sibling = head + 1 - 2 * core
    score_scale = 1.0 / math.sqrt(HEAD_DIM)
    exponent_scale = score_scale * math.log2(math.e)

    def mate(bits):
        other = head
        if bits & SIB:
            other = other + 1 - 2 * core
        if bits & PAIR:
            other = other + 2 - 4 * chip
        return other

    def along(direction, reach):
        return lax.rem(z + (reach if direction == PLUS else n_ctx - reach), n_ctx)

    rows = pl.ds(pl.multiple_of(member * PIECE, PIECE), PIECE)
    cols = pl.ds(pl.multiple_of(group * HEAD_DIM, HEAD_DIM), HEAD_DIM)
    loads = [
        pltpu.make_async_copy(k_hbm.at[rows, cols], kv.at[0, 0, KEY], load_sem.at[0]),
        pltpu.make_async_copy(v_hbm.at[rows, cols], kv.at[0, 0, VAL], load_sem.at[1]),
    ]
    for h in range(2):
        part = pl.ds(h * HEAD_DIM, HEAD_DIM)
        loads.append(pltpu.make_async_copy(q_hbm.at[:, part], q8.at[pl.ds(h * 256, 256)], load_sem.at[2 + h]))
        loads.append(pltpu.make_async_copy(g_hbm.at[:, part], g8.at[pl.ds(h * 256, 256)], load_sem.at[4 + h]))
    for load in loads:
        load.start()

    barrier = pltpu.get_barrier_semaphore()

    def greet(ctx_id, head_id):
        pl.semaphore_signal(barrier, inc=1, device_id=(ctx_id, head_id), device_id_type=MESH)

    for direction in (PLUS, MINUS):
        for reach in range(1, REACH + 1):
            greet(along(direction, reach), head)
    for bits in (SIB, PAIR, DIAG):
        greet(z, mate(bits))
    own_rows = head // 16 == member
    for other in range(QUADS):

        @pl.when(jnp.logical_not(jnp.logical_and(own_rows, quad == other)))
        def _():
            greet(z, other * 4 + head // 16)

    def remote(src, dst, send, recv, ctx_id, head_id):
        return pltpu.make_async_remote_copy(
            src_ref=src,
            dst_ref=dst,
            send_sem=send,
            recv_sem=recv,
            device_id=(ctx_id, head_id),
            device_id_type=MESH,
        )

    def hop(direction, source, reach):
        t = source + reach
        src = kv.at[source, direction if source else 0]
        dst = kv.at[t % half, direction if t < half else 1]
        if t == half:
            kind = KEY if direction == PLUS else VAL
            src, dst = src.at[kind], dst.at[kind]
        return remote(src, dst, kv_send.at[direction, t - 1], kv_recv.at[direction, t - 1], along(direction, reach), head)

    def hops(source, action):
        for reach in range(REACH, 0, -1):
            for direction in (PLUS, MINUS):
                getattr(hop(direction, source, reach), action)()

    def arrived(t):
        for direction in (PLUS, MINUS):
            hop(direction, (t - 1) // REACH * REACH, 1 + (t - 1) % REACH).wait_recv()

    def swap(i, src, dst, bits):
        return remote(src, dst, swap_send.at[i], swap_recv.at[i], z, mate(bits))

    def heads_of(bits):
        return pl.ds(bits * 512, 512)

    q_sib = swap(0, q8.at[heads_of(0)], q8.at[heads_of(SIB)], SIB)
    g_sib = swap(1, g8.at[heads_of(0)], g8.at[heads_of(SIB)], SIB)
    q_pair = swap(2, q8.at[heads_of(0)], q8.at[heads_of(PAIR)], PAIR)
    g_pair = swap(3, g8.at[heads_of(0)], g8.at[heads_of(PAIR)], PAIR)
    q_diag = swap(4, q8.at[heads_of(PAIR)], q8.at[heads_of(DIAG)], SIB)
    g_diag = swap(5, g8.at[heads_of(PAIR)], g8.at[heads_of(DIAG)], SIB)
    stats = [swap(5 + bits, stat, stat_in.at[bits - 1], bits) for bits in (PAIR, DIAG, SIB)]
    mid = swap(9, mid_out, mid_in, SIB)
    last = swap(10, last_out, last_in, PAIR)

    for load in loads[:2]:
        load.wait()
    pl.semaphore_wait(barrier, 2 * REACH + 3 + QUADS - jnp.where(own_rows, 1, 0))
    hops(0, "start")
    for load in loads[2:]:
        load.wait()
    for copy in (q_pair, q_sib, g_pair, g_sib):
        copy.start()

    stat[0:8, :] = jnp.full((8, 256), HIDDEN, F32)
    stat[8:24, :] = jnp.zeros((16, 256), F32)
    rs_in[PLUS, half - 1, VAL] = jnp.zeros((PIECE, HEAD_DIM), BF16)
    rs_in[MINUS, half - 1, KEY] = jnp.zeros((PIECE, HEAD_DIM), BF16)

    def turn(bits):
        for h in range(2):
            at = slice(bits * 512 + h * 256, bits * 512 + (h + 1) * 256)
            q_t[:, at] = q8[at, :].T
            g_t[:, at] = g8[at, :].T

    lane = lax.broadcasted_iota(jnp.int32, (1, 256), 1)
    ahead = (
        lax.rem(lax.broadcasted_iota(jnp.int32, (2 * PIECE, 256), 0), PIECE)
        - lax.rem(lax.broadcasted_iota(jnp.int32, (2 * PIECE, 256), 1), SPAN)
        + core * PIECE
    )
    q_span0 = order_ref[2 * z]
    q_span1 = order_ref[2 * z + 1]

    def forward(t, members):
        def reach_of(block):
            k_span = order_ref[2 * lax.rem(block, n_ctx) + chip]
            reach = jnp.where(lane < SPAN, (q_span0 - k_span) * SPAN, (q_span1 - k_span) * SPAN)
            return jnp.broadcast_to(reach, (PIECE, 256))

        reach = jnp.concatenate([reach_of(z + n_ctx - t), reach_of(z + t + half * (1 // (t + 1)))], axis=0)
        visible = ahead <= reach
        key = jnp.concatenate([kv[t, 0, KEY], kv[t, 1, KEY]], axis=0)
        value = jnp.concatenate([kv[t, 0, VAL], kv[t, 1, VAL]], axis=0)
        for row in [2 * bits + h for bits in members for h in range(2)]:
            at = slice(row * 256, (row + 1) * 256)
            top_at, sum_at, dot_at = [slice(8 * i + row, 8 * i + row + 1) for i in range(3)]
            s = jnp.where(visible, dot(key, q_t[:, at]) * exponent_scale, HIDDEN)
            top = stat[top_at, :]
            new_top = jnp.maximum(top, jnp.max(s, axis=0, keepdims=True))
            p = jnp.exp2(s - new_top)
            dp = dot(value, g_t[:, at])
            shrink = jnp.exp2(top - new_top)
            stat[sum_at, :] = stat[sum_at, :] * shrink + jnp.sum(p, axis=0, keepdims=True)
            stat[dot_at, :] = stat[dot_at, :] * shrink + jnp.sum(p * dp, axis=0, keepdims=True)
            stat[top_at, :] = new_top
            m_blk[t, row : row + 1, :] = new_top
            p_buf[t, :, at] = p
            dp_buf[t, :, at] = dp
        if 0 in members:
            kv_t[KEY, t] = key.T
            kv_t[VAL, t] = value.T

    turn(0)
    q_sib.wait_recv()
    g_sib.wait_recv()
    turn(SIB)
    arrived(REACH)
    hops(REACH, "start")
    arrived(1)
    arrived(2)

    def near_pairs(t, carry):
        forward(t, (0, SIB))

        @pl.when(t == 1)
        def _():
            q_pair.wait_recv()
            q_diag.start()

        return carry

    def near_pairs_mate(t, carry):
        forward(t, (PAIR,))
        return carry

    def far_pairs(i, carry):
        forward((REACH + 1 + i) % half, (0, SIB, PAIR))
        return carry

    def all_pairs_diag(t, carry):
        forward(t, (DIAG,))
        return carry

    lax.fori_loop(1, REACH + 1, near_pairs, 0)
    g_pair.wait_recv()
    g_diag.start()
    turn(PAIR)
    lax.fori_loop(1, REACH + 1, near_pairs_mate, 0)
    for t in range(REACH + 1, half + 1):
        arrived(t)
    lax.fori_loop(0, half - REACH, far_pairs, 0)
    q_diag.wait_recv()
    g_diag.wait_recv()
    turn(DIAG)
    lax.fori_loop(0, half, all_pairs_diag, 0)

    for copy in stats:
        copy.start()
    o_t[...] = jnp.zeros_like(o_t)
    dq_t[...] = jnp.zeros_like(dq_t)
    for copy in stats:
        copy.wait()

    def seen_by(bits, kind):
        if bits == 0:
            return stat[8 * kind : 8 * kind + 8, :]
        order = [8 * kind + 2 * (own ^ bits) for own in range(4)]
        return jnp.concatenate([stat_in[bits - 1, at : at + 2, :] for at in order], axis=0)

    tops = [seen_by(bits, 0) for bits in range(4)]
    top = jnp.maximum(jnp.maximum(tops[0], tops[1]), jnp.maximum(tops[2], tops[3]))
    weights = [jnp.exp2(one - top) for one in tops]
    total = sum(seen_by(bits, 1) * weights[bits] for bits in range(4))
    inverse = 1.0 / total
    both[0] = top
    both[1] = inverse
    both[2] = sum(seen_by(bits, 2) * weights[bits] for bits in range(4)) * inverse

    def grads_of(t):
        factor = jnp.exp2(m_blk[t] - both[0]) * both[1]
        row_dots = both[2]
        for row in range(8):
            at = slice(row * 256, (row + 1) * 256)
            p = p_buf[t, :, at] * factor[row : row + 1]
            pb[:, at] = p.astype(BF16)
            dsb[:, at] = (p * (dp_buf[t, :, at] - row_dots[row : row + 1])).astype(BF16)
        return dot(dsb[...], q8[...]) * score_scale, dot(pb[...], g8[...])

    def rows_add(t):
        for bits in range(4):
            at = slice(bits * 512, (bits + 1) * 512)
            o_t[bits] += dot(kv_t[VAL, t], pb[:, at])
            dq_t[bits] += dot(kv_t[KEY, t], dsb[:, at])

    def pass_on(direction, d):
        src, dst = rs_out.at[direction, d - 1], rs_in.at[direction, d - 1]
        if isinstance(d, int) and d == half:
            kind = KEY if direction == PLUS else VAL
            src, dst = src.at[kind], dst.at[kind]
        reach = (d - 1) % REACH + 1
        return remote(src, dst, rs_send.at[direction, d - 1], rs_recv.at[direction, d - 1], along(direction, reach), head)

    def side(direction):
        return slice(PIECE, 2 * PIECE) if direction == PLUS else slice(0, PIECE)

    grads = grads_of(0)
    for direction, kind in ((PLUS, KEY), (MINUS, VAL)):
        rs_out[direction, half - 1, kind] = grads[kind][PIECE:].astype(BF16)
        pass_on(direction, half).start()
    for kind in (KEY, VAL):
        own_grad[kind] = grads[kind][:PIECE]
    rows_add(0)

    def reduce_step(i, carry):
        d = half - 1 - i - i // 2
        grads = grads_of(d)
        for direction in (PLUS, MINUS):
            for kind in (KEY, VAL):
                rs_out[direction, d - 1, kind] = grads[kind][side(direction)].astype(BF16)
            pass_on(direction, d).start()
        rows_add(d)
        return carry

    lax.fori_loop(0, half - 2, reduce_step, 0)

    grads = grads_of(REACH)
    for kind in (KEY, VAL):
        near_grad[kind] = grads[kind]
    rows_add(REACH)
    for i, bits in enumerate((SIB, DIAG)):
        mid_out[i, 0] = o_t[bits].astype(BF16)
        mid_out[i, 1] = dq_t[bits].astype(BF16)
    mid.start()
    for direction in (PLUS, MINUS):
        for d in range(REACH + 1, half + 1):
            pass_on(direction, d).wait_recv()
        for kind in (KEY, VAL):
            beyond = sum(rs_in[direction, d - 1, kind].astype(F32) for d in range(REACH + 1, half + 1))
            rs_out[direction, REACH - 1, kind] = (near_grad[kind, side(direction), :] + beyond).astype(BF16)
        pass_on(direction, REACH).start()

    mid.wait_recv()
    last_out[0] = (o_t[PAIR] + mid_in[1, 0].astype(F32)).astype(BF16)
    last_out[1] = (dq_t[PAIR] + mid_in[1, 1].astype(F32)).astype(BF16)
    last.start()

    for direction in (PLUS, MINUS):
        for d in range(1, REACH + 1):
            pass_on(direction, d).wait_recv()
    for kind in (KEY, VAL):
        total = own_grad[kind]
        for direction in (PLUS, MINUS):
            for d in range(1, REACH + 1):
                total += rs_in[direction, d - 1, kind].astype(F32)
        for n in range(QUADS):
            f_out[n, 4 * kind : 4 * kind + 4, :] = total[4 * n : 4 * n + 4]

    def to_owner(n):
        return remote(f_out.at[n], f_in.at[quad], f_send.at[n], f_recv.at[0], z, member * 16 + n)

    for n in range(QUADS):
        here = head == member * 16 + n

        @pl.when(here)
        def _():
            pltpu.make_async_copy(f_out.at[n], f_in.at[quad], f_recv.at[0]).start()

        @pl.when(jnp.logical_not(here))
        def _():
            to_owner(n).start()

    last.wait_recv()
    for h in range(2):
        at = slice(h * 256, (h + 1) * 256)
        cols_h = slice(h * HEAD_DIM, (h + 1) * HEAD_DIM)
        for i, part, out, scale in ((0, o_t, o_ref, 1.0), (1, dq_t, dq_ref, score_scale)):
            rows_sum = part[0, :, at] + mid_in[0, i, :, at].astype(F32) + last_in[i, :, at].astype(F32)
            out[:, cols_h] = (rows_sum * scale).T.astype(BF16)

    for copy in (q_sib, g_sib, q_pair, g_pair, q_diag, g_diag, mid, last):
        copy.wait_send()
    for source in range(0, half, REACH):
        hops(source, "wait_send")
    for direction in (PLUS, MINUS):
        for d in range(1, half + 1):
            pass_on(direction, d).wait_send()
    for n in range(QUADS):

        @pl.when(head != member * 16 + n)
        def _():
            to_owner(n).wait_send()

    pltpu.make_async_copy(f_out, f_in, f_recv.at[0]).wait()
    for g in range(QUADS // 2):
        at = slice(g * HEAD_DIM, (g + 1) * HEAD_DIM)
        summed = f_in[2 * g] + f_in[2 * g + 1]
        dk_ref[:, at] = summed[0:4].astype(BF16)
        dv_ref[:, at] = summed[4:8].astype(BF16)


def per_device(query_rows, key_rows, value_rows, out_grad, span_order):
    n_ctx = lax.axis_size("ctx")
    half = n_ctx // 2
    vmem = pltpu.VMEM
    dma = pltpu.SemaphoreType.DMA
    outside = pl.BlockSpec(memory_space=pltpu.HBM)
    local = pl.BlockSpec(memory_space=pltpu.VMEM)
    return pl.pallas_call(
        functools.partial(attention_kernel, n_ctx),
        out_shape=(
            jax.ShapeDtypeStruct((256, 256), BF16),
            jax.ShapeDtypeStruct((256, 256), BF16),
            jax.ShapeDtypeStruct((4, 1024), BF16),
            jax.ShapeDtypeStruct((4, 1024), BF16),
        ),
        in_specs=[pl.BlockSpec(memory_space=pltpu.SMEM), outside, outside, outside, outside],
        out_specs=(local, local, local, local),
        scratch_shapes=[
            vmem((2048, 128), BF16),
            vmem((2048, 128), BF16),
            vmem((128, 2048), BF16),
            vmem((128, 2048), BF16),
            vmem((half, 2, 2, PIECE, 128), BF16),
            vmem((2, half, 128, 128), BF16),
            vmem((half, 128, 2048), F32),
            vmem((half, 128, 2048), F32),
            vmem((half, 8, 256), F32),
            vmem((24, 256), F32),
            vmem((3, 24, 256), F32),
            vmem((3, 8, 256), F32),
            vmem((128, 2048), BF16),
            vmem((128, 2048), BF16),
            vmem((4, 128, 512), F32),
            vmem((4, 128, 512), F32),
            vmem((2, 2, 128, 512), BF16),
            vmem((2, 2, 128, 512), BF16),
            vmem((2, 128, 512), BF16),
            vmem((2, 128, 512), BF16),
            vmem((2, PIECE, 128), F32),
            vmem((2, 2 * PIECE, 128), F32),
            vmem((2, half, 2, PIECE, 128), BF16),
            vmem((2, half, 2, PIECE, 128), BF16),
            vmem((QUADS, 8, 128), F32),
            vmem((QUADS, 8, 128), F32),
            dma((6,)),
            dma((11,)),
            dma((11,)),
            dma((2, half)),
            dma((2, half)),
            dma((2, half)),
            dma((2, half)),
            dma((QUADS,)),
            dma((1,)),
        ],
        compiler_params=pltpu.CompilerParams(
            collective_id=0, has_side_effects=True, vmem_limit_bytes=62 * 1024 * 1024
        ),
    )(span_order, query_rows, key_rows, value_rows, out_grad)


def solution(mesh):
    in_specs = (P("ctx", "head"), P("ctx", None), P("ctx", None), P("ctx", "head"), P())
    out_specs = (
        P("ctx", "head"),
        P("ctx", "head"),
        P(("ctx", "head"), None),
        P(("ctx", "head"), None),
    )
    return jax.shard_map(
        per_device, mesh=mesh, in_specs=in_specs, out_specs=out_specs, check_vma=False
    )
```

```python
import functools
import math

import jax
import jax.numpy as jnp
from jax import lax
from jax.experimental import pallas as pl
from jax.experimental.pallas import tpu as pltpu
from jax.sharding import PartitionSpec as P

HEAD_DIM = 128
SPAN = 128
PIECE = 64
QUADS = 16
HIDDEN = -1e30
F32 = jnp.float32
BF16 = jnp.bfloat16
MESH = pl.DeviceIdType.MESH
PLUS, MINUS = 0, 1
KEY, VAL = 0, 1
SIB, PAIR, DIAG = 1, 2, 3
REACH = 3


def dot(a, b):
    return jnp.dot(a, b, preferred_element_type=F32)


def attention_kernel(
    n_ctx,
    order_ref,
    q_hbm,
    k_hbm,
    v_hbm,
    g_hbm,
    rows_ref,
    grads_ref,
    q8,
    g8,
    q_t,
    g_t,
    kv,
    kv_t,
    p_buf,
    dp_buf,
    m_blk,
    stat,
    stat_in,
    both,
    pb,
    dsb,
    o_t,
    dq_t,
    mid_out,
    mid_in,
    last_out,
    last_in,
    own_grad,
    near_grad,
    rs_in,
    rs_out,
    f_out,
    f_in,
    load_sem,
    swap_send,
    swap_recv,
    kv_send,
    kv_recv,
    rs_send,
    rs_recv,
    f_send,
    f_recv,
):
    half = n_ctx // 2
    z = lax.axis_index("ctx")
    head = lax.axis_index("head")
    group = head // 8
    quad = head // 4
    member = head % 4
    core = head % 2
    chip = member // 2
    sibling = head + 1 - 2 * core
    score_scale = 1.0 / math.sqrt(HEAD_DIM)
    exponent_scale = score_scale * math.log2(math.e)

    def mate(bits):
        other = head
        if bits & SIB:
            other = other + 1 - 2 * core
        if bits & PAIR:
            other = other + 2 - 4 * chip
        return other

    def along(direction, reach):
        return lax.rem(z + (reach if direction == PLUS else n_ctx - reach), n_ctx)

    rows = pl.ds(pl.multiple_of(member * PIECE, PIECE), PIECE)
    cols = pl.ds(pl.multiple_of(group * HEAD_DIM, HEAD_DIM), HEAD_DIM)
    loads = [
        pltpu.make_async_copy(k_hbm.at[rows, cols], kv.at[0, 0, KEY], load_sem.at[0]),
        pltpu.make_async_copy(v_hbm.at[rows, cols], kv.at[0, 0, VAL], load_sem.at[1]),
    ]
    for h in range(2):
        part = pl.ds(h * HEAD_DIM, HEAD_DIM)
        loads.append(pltpu.make_async_copy(q_hbm.at[:, part], q8.at[pl.ds(h * 256, 256)], load_sem.at[2 + h]))
        loads.append(pltpu.make_async_copy(g_hbm.at[:, part], g8.at[pl.ds(h * 256, 256)], load_sem.at[4 + h]))
    for load in loads:
        load.start()

    barrier = pltpu.get_barrier_semaphore()

    def greet(ctx_id, head_id):
        pl.semaphore_signal(barrier, inc=1, device_id=(ctx_id, head_id), device_id_type=MESH)

    for direction in (PLUS, MINUS):
        for reach in range(1, REACH + 1):
            greet(along(direction, reach), head)
    for bits in (SIB, PAIR, DIAG):
        greet(z, mate(bits))
    own_rows = head // 16 == member
    for other in range(QUADS):

        @pl.when(jnp.logical_not(jnp.logical_and(own_rows, quad == other)))
        def _():
            greet(z, other * 4 + head // 16)

    def remote(src, dst, send, recv, ctx_id, head_id):
        return pltpu.make_async_remote_copy(
            src_ref=src,
            dst_ref=dst,
            send_sem=send,
            recv_sem=recv,
            device_id=(ctx_id, head_id),
            device_id_type=MESH,
        )

    def hop(direction, source, reach):
        t = source + reach
        src = kv.at[source, direction if source else 0]
        dst = kv.at[t % half, direction if t < half else 1]
        if t == half:
            kind = KEY if direction == PLUS else VAL
            src, dst = src.at[kind], dst.at[kind]
        return remote(src, dst, kv_send.at[direction, t - 1], kv_recv.at[direction, t - 1], along(direction, reach), head)

    def hops(source, action):
        for reach in range(REACH, 0, -1):
            for direction in (PLUS, MINUS):
                getattr(hop(direction, source, reach), action)()

    def arrived(t):
        for direction in (PLUS, MINUS):
            hop(direction, (t - 1) // REACH * REACH, 1 + (t - 1) % REACH).wait_recv()

    def swap(i, src, dst, bits):
        return remote(src, dst, swap_send.at[i], swap_recv.at[i], z, mate(bits))

    def heads_of(bits):
        return pl.ds(bits * 512, 512)

    q_sib = swap(0, q8.at[heads_of(0)], q8.at[heads_of(SIB)], SIB)
    g_sib = swap(1, g8.at[heads_of(0)], g8.at[heads_of(SIB)], SIB)
    q_pair = swap(2, q8.at[heads_of(0)], q8.at[heads_of(PAIR)], PAIR)
    g_pair = swap(3, g8.at[heads_of(0)], g8.at[heads_of(PAIR)], PAIR)
    q_diag = swap(4, q8.at[heads_of(PAIR)], q8.at[heads_of(DIAG)], SIB)
    g_diag = swap(5, g8.at[heads_of(PAIR)], g8.at[heads_of(DIAG)], SIB)
    stats = [swap(5 + bits, stat, stat_in.at[bits - 1], bits) for bits in (PAIR, DIAG, SIB)]
    mid = swap(9, mid_out, mid_in, SIB)
    last = swap(10, last_out, last_in, PAIR)

    for load in loads[:2]:
        load.wait()
    pl.semaphore_wait(barrier, 2 * REACH + 3 + QUADS - jnp.where(own_rows, 1, 0))
    hops(0, "start")
    for load in loads[2:]:
        load.wait()
    for copy in (q_pair, q_sib, g_pair, g_sib):
        copy.start()

    stat[0:8, :] = jnp.full((8, 256), HIDDEN, F32)
    stat[8:24, :] = jnp.zeros((16, 256), F32)
    rs_in[PLUS, half - 1, VAL] = jnp.zeros((PIECE, HEAD_DIM), BF16)
    rs_in[MINUS, half - 1, KEY] = jnp.zeros((PIECE, HEAD_DIM), BF16)

    def turn(bits):
        for h in range(2):
            at = slice(bits * 512 + h * 256, bits * 512 + (h + 1) * 256)
            q_t[:, at] = q8[at, :].T
            g_t[:, at] = g8[at, :].T

    lane = lax.broadcasted_iota(jnp.int32, (1, 256), 1)
    ahead = (
        lax.rem(lax.broadcasted_iota(jnp.int32, (2 * PIECE, 256), 0), PIECE)
        - lax.rem(lax.broadcasted_iota(jnp.int32, (2 * PIECE, 256), 1), SPAN)
        + core * PIECE
    )
    q_span0 = order_ref[2 * z]
    q_span1 = order_ref[2 * z + 1]

    def span_at(t):
        return pl.ds(t * SPAN if isinstance(t, int) else pl.multiple_of(t * SPAN, SPAN), SPAN)

    def forward(t, members):
        def reach_of(block):
            k_span = order_ref[2 * lax.rem(block, n_ctx) + chip]
            reach = jnp.where(lane < SPAN, (q_span0 - k_span) * SPAN, (q_span1 - k_span) * SPAN)
            return jnp.broadcast_to(reach, (PIECE, 256))

        reach = jnp.concatenate([reach_of(z + n_ctx - t), reach_of(z + t + half * (1 // (t + 1)))], axis=0)
        visible = ahead <= reach
        key = jnp.concatenate([kv[t, 0, KEY], kv[t, 1, KEY]], axis=0)
        value = jnp.concatenate([kv[t, 0, VAL], kv[t, 1, VAL]], axis=0)
        for row in [2 * bits + h for bits in members for h in range(2)]:
            at = slice(row * 256, (row + 1) * 256)
            top_at, sum_at, dot_at = [slice(8 * i + row, 8 * i + row + 1) for i in range(3)]
            s = jnp.where(visible, dot(key, q_t[:, at]) * exponent_scale, HIDDEN)
            top = stat[top_at, :]
            new_top = jnp.maximum(top, jnp.max(s, axis=0, keepdims=True))
            p = jnp.exp2(s - new_top)
            dp = dot(value, g_t[:, at])
            shrink = jnp.exp2(top - new_top)
            stat[sum_at, :] = stat[sum_at, :] * shrink + jnp.sum(p, axis=0, keepdims=True)
            stat[dot_at, :] = stat[dot_at, :] * shrink + jnp.sum(p * dp, axis=0, keepdims=True)
            stat[top_at, :] = new_top
            m_blk[t, row : row + 1, :] = new_top
            p_buf[t, :, at] = p
            dp_buf[t, :, at] = dp
        if 0 in members:
            kv_t[KEY, :, span_at(t)] = key.T
            kv_t[VAL, :, span_at(t)] = value.T

    turn(0)
    q_sib.wait_recv()
    g_sib.wait_recv()
    turn(SIB)
    arrived(REACH)
    hops(REACH, "start")
    arrived(1)
    arrived(2)

    def near_pairs(t, carry):
        forward(t, (0, SIB))

        @pl.when(t == 1)
        def _():
            q_pair.wait_recv()
            q_diag.start()

        return carry

    def near_pairs_mate(t, carry):
        forward(t, (PAIR,))
        return carry

    def near_pairs_diag(t, carry):
        forward(t, (DIAG,))
        return carry

    def far_pairs(i, carry):
        for t in range(REACH + 1, half + 1):

            @pl.when(i == t - REACH - 1)
            def _():
                arrived(t)

        forward((REACH + 1 + i) % half, (0, SIB, PAIR, DIAG))
        return carry

    lax.fori_loop(1, REACH + 1, near_pairs, 0)
    g_pair.wait_recv()
    g_diag.start()
    turn(PAIR)
    lax.fori_loop(1, REACH + 1, near_pairs_mate, 0)
    q_diag.wait_recv()
    g_diag.wait_recv()
    turn(DIAG)
    lax.fori_loop(1, REACH + 1, near_pairs_diag, 0)
    lax.fori_loop(0, half - REACH, far_pairs, 0)

    for copy in stats:
        copy.start()
    for copy in stats:
        copy.wait()

    def seen_by(bits, kind):
        if bits == 0:
            return stat[8 * kind : 8 * kind + 8, :]
        order = [8 * kind + 2 * (own ^ bits) for own in range(4)]
        return jnp.concatenate([stat_in[bits - 1, at : at + 2, :] for at in order], axis=0)

    tops = [seen_by(bits, 0) for bits in range(4)]
    top = jnp.maximum(jnp.maximum(tops[0], tops[1]), jnp.maximum(tops[2], tops[3]))
    weights = [jnp.exp2(one - top) for one in tops]
    total = sum(seen_by(bits, 1) * weights[bits] for bits in range(4))
    inverse = 1.0 / total
    both[0] = top
    both[1] = inverse
    both[2] = sum(seen_by(bits, 2) * weights[bits] for bits in range(4)) * inverse

    def grads_of(t):
        factor = jnp.exp2(m_blk[t] - both[0]) * both[1]
        row_dots = both[2]
        part = span_at(t)
        for row in range(8):
            at = slice(row * 256, (row + 1) * 256)
            p = p_buf[t, :, at] * factor[row : row + 1]
            pb[part, at] = p.astype(BF16)
            dsb[part, at] = (p * (dp_buf[t, :, at] - row_dots[row : row + 1])).astype(BF16)
        return dot(dsb[part, :], q8[...]) * score_scale, dot(pb[part, :], g8[...])

    def rows_of(bits):
        at = slice(bits * 512, (bits + 1) * 512)
        return dot(kv_t[VAL], pb[:, at]), dot(kv_t[KEY], dsb[:, at])

    def pass_on(direction, d):
        src, dst = rs_out.at[direction, d - 1], rs_in.at[direction, d - 1]
        if isinstance(d, int) and d == half:
            kind = KEY if direction == PLUS else VAL
            src, dst = src.at[kind], dst.at[kind]
        reach = (d - 1) % REACH + 1
        return remote(src, dst, rs_send.at[direction, d - 1], rs_recv.at[direction, d - 1], along(direction, reach), head)

    def side(direction):
        return slice(PIECE, 2 * PIECE) if direction == PLUS else slice(0, PIECE)

    grads = grads_of(0)
    for direction, kind in ((PLUS, KEY), (MINUS, VAL)):
        rs_out[direction, half - 1, kind] = grads[kind][PIECE:].astype(BF16)
        pass_on(direction, half).start()
    for kind in (KEY, VAL):
        own_grad[kind] = grads[kind][:PIECE]

    def reduce_step(i, carry):
        d = half - 1 - i - i // 2
        grads = grads_of(d)
        for direction in (PLUS, MINUS):
            for kind in (KEY, VAL):
                rs_out[direction, d - 1, kind] = grads[kind][side(direction)].astype(BF16)
            pass_on(direction, d).start()
        return carry

    lax.fori_loop(0, half - 2, reduce_step, 0)

    grads = grads_of(REACH)
    for kind in (KEY, VAL):
        near_grad[kind] = grads[kind]
    for i, bits in enumerate((SIB, DIAG)):
        for j, rows_sum in enumerate(rows_of(bits)):
            mid_out[i, j] = rows_sum.astype(BF16)
    mid.start()
    for i, bits in enumerate((0, PAIR)):
        o_t[i], dq_t[i] = rows_of(bits)
    for direction in (PLUS, MINUS):
        for d in range(REACH + 1, half + 1):
            pass_on(direction, d).wait_recv()
        for kind in (KEY, VAL):
            beyond = sum(rs_in[direction, d - 1, kind].astype(F32) for d in range(REACH + 1, half + 1))
            rs_out[direction, REACH - 1, kind] = (near_grad[kind, side(direction), :] + beyond).astype(BF16)
        pass_on(direction, REACH).start()

    mid.wait_recv()
    last_out[0] = (o_t[1] + mid_in[1, 0].astype(F32)).astype(BF16)
    last_out[1] = (dq_t[1] + mid_in[1, 1].astype(F32)).astype(BF16)
    last.start()

    for direction in (PLUS, MINUS):
        for d in range(1, REACH + 1):
            pass_on(direction, d).wait_recv()
    for kind in (KEY, VAL):
        total = own_grad[kind]
        for direction in (PLUS, MINUS):
            for d in range(1, REACH + 1):
                total += rs_in[direction, d - 1, kind].astype(F32)
        for n in range(QUADS):
            f_out[n, 4 * kind : 4 * kind + 4, :] = total[4 * n : 4 * n + 4]

    def to_owner(n):
        return remote(f_out.at[n], f_in.at[quad], f_send.at[n], f_recv.at[0], z, member * 16 + n)

    for n in range(QUADS):
        here = head == member * 16 + n

        @pl.when(here)
        def _():
            pltpu.make_async_copy(f_out.at[n], f_in.at[quad], f_recv.at[0]).start()

        @pl.when(jnp.logical_not(here))
        def _():
            to_owner(n).start()

    last.wait_recv()
    for h in range(2):
        at = slice(h * 256, (h + 1) * 256)
        cols_h = slice(h * HEAD_DIM, (h + 1) * HEAD_DIM)
        for i, part, out, scale in ((0, o_t, rows_ref.at[0], 1.0), (1, dq_t, rows_ref.at[1], score_scale)):
            rows_sum = part[0, :, at] + mid_in[0, i, :, at].astype(F32) + last_in[i, :, at].astype(F32)
            out[:, cols_h] = (rows_sum * scale).T.astype(BF16)

    for copy in (q_sib, g_sib, q_pair, g_pair, q_diag, g_diag, mid, last):
        copy.wait_send()
    for source in range(0, half, REACH):
        hops(source, "wait_send")
    for direction in (PLUS, MINUS):
        for d in range(1, half + 1):
            pass_on(direction, d).wait_send()
    for n in range(QUADS):

        @pl.when(head != member * 16 + n)
        def _():
            to_owner(n).wait_send()

    pltpu.make_async_copy(f_out, f_in, f_recv.at[0]).wait()
    for g in range(QUADS // 2):
        at = slice(g * HEAD_DIM, (g + 1) * HEAD_DIM)
        summed = f_in[2 * g] + f_in[2 * g + 1]
        grads_ref[:, at] = summed.astype(BF16)


def per_device(query_rows, key_rows, value_rows, out_grad, span_order):
    n_ctx = lax.axis_size("ctx")
    half = n_ctx // 2
    vmem = pltpu.VMEM
    dma = pltpu.SemaphoreType.DMA
    outside = pl.BlockSpec(memory_space=pltpu.HBM)
    local = pl.BlockSpec(memory_space=pltpu.VMEM)
    rows, grads = pl.pallas_call(
        functools.partial(attention_kernel, n_ctx),
        out_shape=(
            jax.ShapeDtypeStruct((2, 256, 256), BF16),
            jax.ShapeDtypeStruct((8, 1024), BF16),
        ),
        in_specs=[pl.BlockSpec(memory_space=pltpu.SMEM), outside, outside, outside, outside],
        out_specs=(local, local),
        scratch_shapes=[
            vmem((2048, 128), BF16),
            vmem((2048, 128), BF16),
            vmem((128, 2048), BF16),
            vmem((128, 2048), BF16),
            vmem((half, 2, 2, PIECE, 128), BF16),
            vmem((2, 128, half * 128), BF16),
            vmem((half, 128, 2048), F32),
            vmem((half, 128, 2048), F32),
            vmem((half, 8, 256), F32),
            vmem((24, 256), F32),
            vmem((3, 24, 256), F32),
            vmem((3, 8, 256), F32),
            vmem((half * 128, 2048), BF16),
            vmem((half * 128, 2048), BF16),
            vmem((2, 128, 512), F32),
            vmem((2, 128, 512), F32),
            vmem((2, 2, 128, 512), BF16),
            vmem((2, 2, 128, 512), BF16),
            vmem((2, 128, 512), BF16),
            vmem((2, 128, 512), BF16),
            vmem((2, PIECE, 128), F32),
            vmem((2, 2 * PIECE, 128), F32),
            vmem((2, half, 2, PIECE, 128), BF16),
            vmem((2, half, 2, PIECE, 128), BF16),
            vmem((QUADS, 8, 128), F32),
            vmem((QUADS, 8, 128), F32),
            dma((6,)),
            dma((11,)),
            dma((11,)),
            dma((2, half)),
            dma((2, half)),
            dma((2, half)),
            dma((2, half)),
            dma((QUADS,)),
            dma((1,)),
        ],
        compiler_params=pltpu.CompilerParams(
            collective_id=0, has_side_effects=True, vmem_limit_bytes=62 * 1024 * 1024
        ),
    )(span_order, query_rows, key_rows, value_rows, out_grad)
    return rows[0], rows[1], grads[:4], grads[4:]


def solution(mesh):
    in_specs = (P("ctx", "head"), P("ctx", None), P("ctx", None), P("ctx", "head"), P())
    out_specs = (
        P("ctx", "head"),
        P("ctx", "head"),
        P(("ctx", "head"), None),
        P(("ctx", "head"), None),
    )
    return jax.shard_map(
        per_device, mesh=mesh, in_specs=in_specs, out_specs=out_specs, check_vma=False
    )
```

```python
import functools
import math

import jax
import jax.numpy as jnp
from jax import lax
from jax.experimental import pallas as pl
from jax.experimental.pallas import tpu as pltpu
from jax.sharding import PartitionSpec as P

HEAD_DIM = 128
SPAN = 128
PIECE = 64
QUADS = 16
HIDDEN = -1e30
F32 = jnp.float32
BF16 = jnp.bfloat16
MESH = pl.DeviceIdType.MESH
PLUS, MINUS = 0, 1
KEY, VAL = 0, 1
SIB, PAIR, DIAG = 1, 2, 3
REACH = 3


def dot(a, b):
    return jnp.dot(a, b, preferred_element_type=F32)


def attention_kernel(
    n_ctx,
    order_ref,
    q_hbm,
    k_hbm,
    v_hbm,
    g_hbm,
    rows_ref,
    grads_ref,
    q8,
    g8,
    q_t,
    g_t,
    bias,
    kv,
    kv_t,
    p_buf,
    dp_buf,
    m_blk,
    stat,
    stat_in,
    both,
    pb,
    dsb,
    o_t,
    dq_t,
    mid_out,
    mid_in,
    last_out,
    last_in,
    own_grad,
    near_grad,
    rs_in,
    rs_out,
    f_out,
    f_in,
    load_sem,
    swap_send,
    swap_recv,
    kv_send,
    kv_recv,
    rs_send,
    rs_recv,
    f_send,
    f_recv,
    word_sem,
):
    half = n_ctx // 2
    z = lax.axis_index("ctx")
    head = lax.axis_index("head")
    group = head // 8
    quad = head // 4
    member = head % 4
    core = head % 2
    chip = member // 2
    sibling = head + 1 - 2 * core
    score_scale = 1.0 / math.sqrt(HEAD_DIM)
    exponent_scale = score_scale * math.log2(math.e)

    def mate(bits):
        other = head
        if bits & SIB:
            other = other + 1 - 2 * core
        if bits & PAIR:
            other = other + 2 - 4 * chip
        return other

    def along(direction, reach):
        return lax.rem(z + (reach if direction == PLUS else n_ctx - reach), n_ctx)

    rows = pl.ds(pl.multiple_of(member * PIECE, PIECE), PIECE)
    cols = pl.ds(pl.multiple_of(group * HEAD_DIM, HEAD_DIM), HEAD_DIM)
    loads = [
        pltpu.make_async_copy(k_hbm.at[rows, cols], kv.at[0, 0, KEY], load_sem.at[0]),
        pltpu.make_async_copy(v_hbm.at[rows, cols], kv.at[0, 0, VAL], load_sem.at[1]),
    ]
    for h in range(2):
        part = pl.ds(h * HEAD_DIM, HEAD_DIM)
        loads.append(pltpu.make_async_copy(q_hbm.at[:, part], q8.at[pl.ds(h * 256, 256)], load_sem.at[2 + h]))
        loads.append(pltpu.make_async_copy(g_hbm.at[:, part], g8.at[pl.ds(h * 256, 256)], load_sem.at[4 + h]))
    for load in loads:
        load.start()

    barrier = pltpu.get_barrier_semaphore()

    def greet(ctx_id, head_id):
        pl.semaphore_signal(barrier, inc=1, device_id=(ctx_id, head_id), device_id_type=MESH)

    for direction in (PLUS, MINUS):
        for reach in range(1, REACH + 1):
            greet(along(direction, reach), head)
    for bits in (SIB, PAIR, DIAG):
        greet(z, mate(bits))
    column = head // 16
    place = quad % 4
    speaks = column == member

    def speaker(step):
        return column * 16 + lax.rem(place + step, 4) * 4 + member

    @pl.when(speaks)
    def _():
        greet(z, speaker(1))
        greet(z, speaker(3))

    @pl.when(jnp.logical_not(speaks))
    def _():
        greet(z, member * 16 + place * 4 + member)

    def word(sem, head_id):
        pl.semaphore_signal(sem, inc=1, device_id=(z, head_id), device_id_type=MESH)

    def remote(src, dst, send, recv, ctx_id, head_id):
        return pltpu.make_async_remote_copy(
            src_ref=src,
            dst_ref=dst,
            send_sem=send,
            recv_sem=recv,
            device_id=(ctx_id, head_id),
            device_id_type=MESH,
        )

    def hop(direction, source, reach):
        t = source + reach
        src = kv.at[source, direction if source else 0]
        dst = kv.at[t % half, direction if t < half else 1]
        if t == half:
            kind = KEY if direction == PLUS else VAL
            src, dst = src.at[kind], dst.at[kind]
        return remote(src, dst, kv_send.at[direction, t - 1], kv_recv.at[direction, t - 1], along(direction, reach), head)

    def hops(source, action):
        for reach in range(REACH, 0, -1):
            for direction in (PLUS, MINUS):
                getattr(hop(direction, source, reach), action)()

    def arrived(t):
        for direction in (PLUS, MINUS):
            hop(direction, (t - 1) // REACH * REACH, 1 + (t - 1) % REACH).wait_recv()

    def swap(i, src, dst, bits):
        return remote(src, dst, swap_send.at[i], swap_recv.at[i], z, mate(bits))

    def heads_of(bits):
        return pl.ds(bits * 512, 512)

    q_sib = swap(0, q8.at[heads_of(0)], q8.at[heads_of(SIB)], SIB)
    g_sib = swap(1, g8.at[heads_of(0)], g8.at[heads_of(SIB)], SIB)
    q_pair = swap(2, q8.at[heads_of(0)], q8.at[heads_of(PAIR)], PAIR)
    g_pair = swap(3, g8.at[heads_of(0)], g8.at[heads_of(PAIR)], PAIR)
    q_diag = swap(4, q8.at[heads_of(PAIR)], q8.at[heads_of(DIAG)], SIB)
    g_diag = swap(5, g8.at[heads_of(PAIR)], g8.at[heads_of(DIAG)], SIB)
    stats = [swap(5 + bits, stat, stat_in.at[bits - 1], bits) for bits in (PAIR, DIAG, SIB)]
    mid = swap(9, mid_out, mid_in, SIB)
    last = swap(10, last_out, last_in, PAIR)

    for load in loads[:2]:
        load.wait()
    pl.semaphore_wait(barrier, 2 * REACH + 3 + jnp.where(speaks, 5, 0))
    hops(0, "start")
    for load in loads[2:]:
        load.wait()
    for copy in (q_pair, q_sib, g_pair, g_sib):
        copy.start()

    @pl.when(speaks)
    def _():
        word(word_sem.at[0], speaker(1))
        word(word_sem.at[0], speaker(3))

    stat[0:8, :] = jnp.full((8, 256), HIDDEN, F32)
    stat[8:24, :] = jnp.zeros((16, 256), F32)
    rs_in[PLUS, half - 1, VAL] = jnp.zeros((PIECE, HEAD_DIM), BF16)
    rs_in[MINUS, half - 1, KEY] = jnp.zeros((PIECE, HEAD_DIM), BF16)

    def turn(bits):
        for h in range(2):
            at = slice(bits * 512 + h * 256, bits * 512 + (h + 1) * 256)
            q_t[:, at] = q8[at, :].T
            g_t[:, at] = g8[at, :].T

    lane = lax.broadcasted_iota(jnp.int32, (1, 256), 1)
    ahead = (
        lax.rem(lax.broadcasted_iota(jnp.int32, (2 * PIECE, 256), 0), PIECE)
        - lax.rem(lax.broadcasted_iota(jnp.int32, (2 * PIECE, 256), 1), SPAN)
        + core * PIECE
    )
    q_span0 = order_ref[2 * z]
    q_span1 = order_ref[2 * z + 1]

    def span_at(place):
        return pl.ds(place * SPAN if isinstance(place, int) else pl.multiple_of(place * SPAN, SPAN), SPAN)

    def reach_at(t):
        def reach_of(block):
            k_span = order_ref[2 * lax.rem(block, n_ctx) + chip]
            reach = jnp.where(lane < SPAN, (q_span0 - k_span) * SPAN, (q_span1 - k_span) * SPAN)
            return jnp.broadcast_to(reach, (PIECE, 256))

        return jnp.concatenate([reach_of(z + n_ctx - t), reach_of(z + t + half * (1 // (t + 1)))], axis=0)

    def forward(t, members, place):
        visible = ahead <= reach_at(t)
        key = jnp.concatenate([kv[t, 0, KEY], kv[t, 1, KEY]], axis=0)
        value = jnp.concatenate([kv[t, 0, VAL], kv[t, 1, VAL]], axis=0)
        for row in [2 * bits + h for bits in members for h in range(2)]:
            at = slice(row * 256, (row + 1) * 256)
            top_at, sum_at, dot_at = [slice(8 * i + row, 8 * i + row + 1) for i in range(3)]
            s = jnp.where(visible, dot(key, q_t[:, at]) * exponent_scale, HIDDEN)
            top = stat[top_at, :]
            new_top = jnp.maximum(top, jnp.max(s, axis=0, keepdims=True))
            p = jnp.exp2(s - new_top)
            dp = dot(value, g_t[:, at])
            shrink = jnp.exp2(top - new_top)
            stat[sum_at, :] = stat[sum_at, :] * shrink + jnp.sum(p, axis=0, keepdims=True)
            stat[dot_at, :] = stat[dot_at, :] * shrink + jnp.sum(p * dp, axis=0, keepdims=True)
            stat[top_at, :] = new_top
            m_blk[t, row : row + 1, :] = new_top
            p_buf[t, :, at] = p
            dp_buf[t, :, at] = dp
        if 0 in members:
            kv_t[KEY, :, span_at(place)] = key.T
            kv_t[VAL, :, span_at(place)] = value.T

    turn(0)
    q_sib.wait_recv()
    g_sib.wait_recv()
    turn(SIB)
    arrived(REACH)
    hops(REACH, "start")
    arrived(1)
    arrived(2)

    def near_pairs(t, carry):
        forward(t, (0, SIB), t)

        @pl.when(t == 1)
        def _():
            q_pair.wait_recv()
            q_diag.start()

        return carry

    def near_pairs_mate(t, carry):
        forward(t, (PAIR,), t)
        return carry

    def near_pairs_diag(t, carry):
        forward(t, (DIAG,), t)
        return carry

    far = (0, half - 1, half - 2)

    def far_bias():
        for i, t in enumerate(far):
            bias[span_at(i), :] = jnp.where(ahead <= reach_at(t), 0.0, HIDDEN)

    def far_pairs():
        def joined(kind):
            return jnp.concatenate([kv[t, side, kind] for t in far for side in range(2)], axis=0)

        key, value = joined(KEY), joined(VAL)
        for row in range(8):
            at = slice(row * 256, (row + 1) * 256)
            top_at, sum_at, dot_at = [slice(8 * i + row, 8 * i + row + 1) for i in range(3)]
            s = dot(key, q_t[:, at]) * exponent_scale + bias[...]
            top = stat[top_at, :]
            new_top = jnp.maximum(top, jnp.max(s, axis=0, keepdims=True))
            p = jnp.exp2(s - new_top)
            dp = dot(value, g_t[:, at])
            shrink = jnp.exp2(top - new_top)
            stat[sum_at, :] = stat[sum_at, :] * shrink + jnp.sum(p, axis=0, keepdims=True)
            stat[dot_at, :] = stat[dot_at, :] * shrink + jnp.sum(p * dp, axis=0, keepdims=True)
            stat[top_at, :] = new_top
            for i, t in enumerate(far):
                m_blk[t, row : row + 1, :] = new_top
                p_buf[t, :, at] = p[i * SPAN : (i + 1) * SPAN]
                dp_buf[t, :, at] = dp[i * SPAN : (i + 1) * SPAN]

    def far_turn():
        for t in far:
            for kind in (KEY, VAL):
                kv_t[kind, :, span_at(t)] = jnp.concatenate([kv[t, 0, kind], kv[t, 1, kind]], axis=0).T

    lax.fori_loop(1, REACH + 1, near_pairs, 0)

    @pl.when(speaks)
    def _():
        pl.semaphore_wait(word_sem.at[0], 2)
        word(word_sem.at[1], speaker(1))

    g_pair.wait_recv()
    g_diag.start()
    turn(PAIR)
    lax.fori_loop(1, REACH + 1, near_pairs_mate, 0)
    q_diag.wait_recv()
    g_diag.wait_recv()
    turn(DIAG)

    @pl.when(speaks)
    def _():
        pl.semaphore_wait(word_sem.at[1], 1)
        for step in range(1, 4):
            word(word_sem.at[2], lax.rem(column + step, 4) * 16 + place * 4 + member)

    lax.fori_loop(1, REACH + 1, near_pairs_diag, 0)
    far_bias()
    for t in range(REACH + 1, half + 1):
        arrived(t)
    far_pairs()

    for copy in stats:
        copy.start()
    far_turn()
    for copy in stats:
        copy.wait()

    def seen_by(bits, kind):
        if bits == 0:
            return stat[8 * kind : 8 * kind + 8, :]
        order = [8 * kind + 2 * (own ^ bits) for own in range(4)]
        return jnp.concatenate([stat_in[bits - 1, at : at + 2, :] for at in order], axis=0)

    tops = [seen_by(bits, 0) for bits in range(4)]
    top = jnp.maximum(jnp.maximum(tops[0], tops[1]), jnp.maximum(tops[2], tops[3]))
    weights = [jnp.exp2(one - top) for one in tops]
    total = sum(seen_by(bits, 1) * weights[bits] for bits in range(4))
    inverse = 1.0 / total
    both[0] = top
    both[1] = inverse
    both[2] = sum(seen_by(bits, 2) * weights[bits] for bits in range(4)) * inverse

    def grads_of(t):
        factor = jnp.exp2(m_blk[t] - both[0]) * both[1]
        row_dots = both[2]
        part = span_at(t)
        for row in range(8):
            at = slice(row * 256, (row + 1) * 256)
            p = p_buf[t, :, at] * factor[row : row + 1]
            pb[part, at] = p.astype(BF16)
            dsb[part, at] = (p * (dp_buf[t, :, at] - row_dots[row : row + 1])).astype(BF16)
        return dot(dsb[part, :], q8[...]) * score_scale, dot(pb[part, :], g8[...])

    def rows_of(bits):
        at = slice(bits * 512, (bits + 1) * 512)
        return dot(kv_t[VAL], pb[:, at]), dot(kv_t[KEY], dsb[:, at])

    def pass_on(direction, d):
        src, dst = rs_out.at[direction, d - 1], rs_in.at[direction, d - 1]
        if isinstance(d, int) and d == half:
            kind = KEY if direction == PLUS else VAL
            src, dst = src.at[kind], dst.at[kind]
        reach = (d - 1) % REACH + 1
        return remote(src, dst, rs_send.at[direction, d - 1], rs_recv.at[direction, d - 1], along(direction, reach), head)

    def side(direction):
        return slice(PIECE, 2 * PIECE) if direction == PLUS else slice(0, PIECE)

    grads = grads_of(0)
    for direction, kind in ((PLUS, KEY), (MINUS, VAL)):
        rs_out[direction, half - 1, kind] = grads[kind][PIECE:].astype(BF16)
        pass_on(direction, half).start()
    for kind in (KEY, VAL):
        own_grad[kind] = grads[kind][:PIECE]

    def reduce_step(i, carry):
        d = half - 1 - i - i // 2
        grads = grads_of(d)
        for direction in (PLUS, MINUS):
            for kind in (KEY, VAL):
                rs_out[direction, d - 1, kind] = grads[kind][side(direction)].astype(BF16)
            pass_on(direction, d).start()
        return carry

    lax.fori_loop(0, half - 2, reduce_step, 0)

    grads = grads_of(REACH)
    for kind in (KEY, VAL):
        near_grad[kind] = grads[kind]
    for i, bits in enumerate((SIB, DIAG)):
        for j, rows_sum in enumerate(rows_of(bits)):
            mid_out[i, j] = rows_sum.astype(BF16)
    mid.start()
    for i, bits in enumerate((0, PAIR)):
        o_t[i], dq_t[i] = rows_of(bits)
    for direction in (PLUS, MINUS):
        for d in range(REACH + 1, half + 1):
            pass_on(direction, d).wait_recv()
        for kind in (KEY, VAL):
            beyond = sum(rs_in[direction, d - 1, kind].astype(F32) for d in range(REACH + 1, half + 1))
            rs_out[direction, REACH - 1, kind] = (near_grad[kind, side(direction), :] + beyond).astype(BF16)
        pass_on(direction, REACH).start()

    mid.wait_recv()
    last_out[0] = (o_t[1] + mid_in[1, 0].astype(F32)).astype(BF16)
    last_out[1] = (dq_t[1] + mid_in[1, 1].astype(F32)).astype(BF16)
    last.start()

    @pl.when(jnp.logical_not(speaks))
    def _():
        pl.semaphore_wait(word_sem.at[2], 1)

    for direction in (PLUS, MINUS):
        for d in range(1, REACH + 1):
            pass_on(direction, d).wait_recv()
    for kind in (KEY, VAL):
        total = own_grad[kind]
        for direction in (PLUS, MINUS):
            for d in range(1, REACH + 1):
                total += rs_in[direction, d - 1, kind].astype(F32)
        for n in range(QUADS):
            f_out[n, 4 * kind : 4 * kind + 4, :] = total[4 * n : 4 * n + 4]

    def to_owner(n):
        return remote(f_out.at[n], f_in.at[quad], f_send.at[n], f_recv.at[0], z, member * 16 + n)

    for n in range(QUADS):
        here = head == member * 16 + n

        @pl.when(here)
        def _():
            pltpu.make_async_copy(f_out.at[n], f_in.at[quad], f_recv.at[0]).start()

        @pl.when(jnp.logical_not(here))
        def _():
            to_owner(n).start()

    last.wait_recv()
    for h in range(2):
        at = slice(h * 256, (h + 1) * 256)
        cols_h = slice(h * HEAD_DIM, (h + 1) * HEAD_DIM)
        for i, part, out, scale in ((0, o_t, rows_ref.at[0], 1.0), (1, dq_t, rows_ref.at[1], score_scale)):
            rows_sum = part[0, :, at] + mid_in[0, i, :, at].astype(F32) + last_in[i, :, at].astype(F32)
            out[:, cols_h] = (rows_sum * scale).T.astype(BF16)

    for copy in (q_sib, g_sib, q_pair, g_pair, q_diag, g_diag, mid, last):
        copy.wait_send()
    for source in range(0, half, REACH):
        hops(source, "wait_send")
    for direction in (PLUS, MINUS):
        for d in range(1, half + 1):
            pass_on(direction, d).wait_send()
    for n in range(QUADS):

        @pl.when(head != member * 16 + n)
        def _():
            to_owner(n).wait_send()

    pltpu.make_async_copy(f_out, f_in, f_recv.at[0]).wait()
    for g in range(QUADS // 2):
        at = slice(g * HEAD_DIM, (g + 1) * HEAD_DIM)
        summed = f_in[2 * g] + f_in[2 * g + 1]
        grads_ref[:, at] = summed.astype(BF16)


def per_device(query_rows, key_rows, value_rows, out_grad, span_order):
    n_ctx = lax.axis_size("ctx")
    half = n_ctx // 2
    vmem = pltpu.VMEM
    dma = pltpu.SemaphoreType.DMA
    outside = pl.BlockSpec(memory_space=pltpu.HBM)
    local = pl.BlockSpec(memory_space=pltpu.VMEM)
    rows, grads = pl.pallas_call(
        functools.partial(attention_kernel, n_ctx),
        out_shape=(
            jax.ShapeDtypeStruct((2, 256, 256), BF16),
            jax.ShapeDtypeStruct((8, 1024), BF16),
        ),
        in_specs=[pl.BlockSpec(memory_space=pltpu.SMEM), outside, outside, outside, outside],
        out_specs=(local, local),
        scratch_shapes=[
            vmem((2048, 128), BF16),
            vmem((2048, 128), BF16),
            vmem((128, 2048), BF16),
            vmem((128, 2048), BF16),
            vmem((3 * SPAN, 256), F32),
            vmem((half, 2, 2, PIECE, 128), BF16),
            vmem((2, 128, half * 128), BF16),
            vmem((half, 128, 2048), F32),
            vmem((half, 128, 2048), F32),
            vmem((half, 8, 256), F32),
            vmem((24, 256), F32),
            vmem((3, 24, 256), F32),
            vmem((3, 8, 256), F32),
            vmem((half * 128, 2048), BF16),
            vmem((half * 128, 2048), BF16),
            vmem((2, 128, 512), F32),
            vmem((2, 128, 512), F32),
            vmem((2, 2, 128, 512), BF16),
            vmem((2, 2, 128, 512), BF16),
            vmem((2, 128, 512), BF16),
            vmem((2, 128, 512), BF16),
            vmem((2, PIECE, 128), F32),
            vmem((2, 2 * PIECE, 128), F32),
            vmem((2, half, 2, PIECE, 128), BF16),
            vmem((2, half, 2, PIECE, 128), BF16),
            vmem((QUADS, 8, 128), F32),
            vmem((QUADS, 8, 128), F32),
            dma((6,)),
            dma((11,)),
            dma((11,)),
            dma((2, half)),
            dma((2, half)),
            dma((2, half)),
            dma((2, half)),
            dma((QUADS,)),
            dma((1,)),
            pltpu.SemaphoreType.REGULAR((3,)),
        ],
        compiler_params=pltpu.CompilerParams(
            collective_id=0, has_side_effects=True, vmem_limit_bytes=62 * 1024 * 1024
        ),
    )(span_order, query_rows, key_rows, value_rows, out_grad)
    return rows[0], rows[1], grads[:4], grads[4:]


def solution(mesh):
    in_specs = (P("ctx", "head"), P("ctx", None), P("ctx", None), P("ctx", "head"), P())
    out_specs = (
        P("ctx", "head"),
        P("ctx", "head"),
        P(("ctx", "head"), None),
        P(("ctx", "head"), None),
    )
    return jax.shard_map(
        per_device, mesh=mesh, in_specs=in_specs, out_specs=out_specs, check_vma=False
    )
```

```python
import functools
import math

import jax
import jax.numpy as jnp
from jax import lax
from jax.experimental import pallas as pl
from jax.experimental.pallas import tpu as pltpu
from jax.sharding import PartitionSpec as P

HEAD_DIM = 128
SPAN = 128
PIECE = 64
QUADS = 16
HIDDEN = -1e30
F32 = jnp.float32
BF16 = jnp.bfloat16
MESH = pl.DeviceIdType.MESH
PLUS, MINUS = 0, 1
KEY, VAL = 0, 1
SIB, PAIR, DIAG = 1, 2, 3
REACH = 3


def dot(a, b):
    return jnp.dot(a, b, preferred_element_type=F32)


def attention_kernel(
    n_ctx,
    order_ref,
    q_hbm,
    k_hbm,
    v_hbm,
    g_hbm,
    rows_ref,
    grads_ref,
    q8,
    g8,
    q_t,
    g_t,
    bias,
    kv,
    kv_t,
    p_buf,
    dp_buf,
    m_blk,
    stat,
    stat_in,
    both,
    pb,
    dsb,
    o_t,
    dq_t,
    mid_out,
    mid_in,
    last_out,
    last_in,
    own_grad,
    near_grad,
    rs_in,
    rs_out,
    f_out,
    f_in,
    load_sem,
    swap_send,
    swap_recv,
    kv_send,
    kv_recv,
    rs_send,
    rs_recv,
    f_send,
    f_recv,
    word_sem,
):
    half = n_ctx // 2
    z = lax.axis_index("ctx")
    head = lax.axis_index("head")
    group = head // 8
    quad = head // 4
    member = head % 4
    core = head % 2
    chip = member // 2
    sibling = head + 1 - 2 * core
    score_scale = 1.0 / math.sqrt(HEAD_DIM)
    exponent_scale = score_scale * math.log2(math.e)

    def mate(bits):
        other = head
        if bits & SIB:
            other = other + 1 - 2 * core
        if bits & PAIR:
            other = other + 2 - 4 * chip
        return other

    def along(direction, reach):
        return lax.rem(z + (reach if direction == PLUS else n_ctx - reach), n_ctx)

    rows = pl.ds(pl.multiple_of(member * PIECE, PIECE), PIECE)
    cols = pl.ds(pl.multiple_of(group * HEAD_DIM, HEAD_DIM), HEAD_DIM)
    loads = [
        pltpu.make_async_copy(k_hbm.at[rows, cols], kv.at[0, 0, KEY], load_sem.at[0]),
        pltpu.make_async_copy(v_hbm.at[rows, cols], kv.at[0, 0, VAL], load_sem.at[1]),
    ]
    for h in range(2):
        part = pl.ds(h * HEAD_DIM, HEAD_DIM)
        loads.append(pltpu.make_async_copy(q_hbm.at[:, part], q8.at[pl.ds(h * 256, 256)], load_sem.at[2 + h]))
        loads.append(pltpu.make_async_copy(g_hbm.at[:, part], g8.at[pl.ds(h * 256, 256)], load_sem.at[4 + h]))
    for load in loads:
        load.start()

    barrier = pltpu.get_barrier_semaphore()

    def greet(ctx_id, head_id):
        pl.semaphore_signal(barrier, inc=1, device_id=(ctx_id, head_id), device_id_type=MESH)

    for reach in range(REACH, 0, -1):
        for direction in (PLUS, MINUS):
            greet(along(direction, reach), head)
    for bits in (SIB, PAIR, DIAG):
        greet(z, mate(bits))
    column = head // 16
    place = quad % 4
    speaks = column == member

    def speaker(step):
        return column * 16 + lax.rem(place + step, 4) * 4 + member

    @pl.when(speaks)
    def _():
        greet(z, speaker(1))
        greet(z, speaker(3))

    @pl.when(jnp.logical_not(speaks))
    def _():
        greet(z, member * 16 + place * 4 + member)

    def word(sem, head_id):
        pl.semaphore_signal(sem, inc=1, device_id=(z, head_id), device_id_type=MESH)

    def remote(src, dst, send, recv, ctx_id, head_id):
        return pltpu.make_async_remote_copy(
            src_ref=src,
            dst_ref=dst,
            send_sem=send,
            recv_sem=recv,
            device_id=(ctx_id, head_id),
            device_id_type=MESH,
        )

    def hop(direction, source, reach):
        t = source + reach
        src = kv.at[source, direction if source else 0]
        dst = kv.at[t % half, direction if t < half else 1]
        if t == half:
            kind = KEY if direction == PLUS else VAL
            src, dst = src.at[kind], dst.at[kind]
        return remote(src, dst, kv_send.at[direction, t - 1], kv_recv.at[direction, t - 1], along(direction, reach), head)

    def hops(source, action):
        for reach in range(REACH, 0, -1):
            for direction in (PLUS, MINUS):
                getattr(hop(direction, source, reach), action)()

    def arrived(t):
        for direction in (PLUS, MINUS):
            hop(direction, (t - 1) // REACH * REACH, 1 + (t - 1) % REACH).wait_recv()

    def swap(i, src, dst, bits):
        return remote(src, dst, swap_send.at[i], swap_recv.at[i], z, mate(bits))

    def heads_of(bits):
        return pl.ds(bits * 512, 512)

    q_sib = swap(0, q8.at[heads_of(0)], q8.at[heads_of(SIB)], SIB)
    g_sib = swap(1, g8.at[heads_of(0)], g8.at[heads_of(SIB)], SIB)
    q_pair = swap(2, q8.at[heads_of(0)], q8.at[heads_of(PAIR)], PAIR)
    g_pair = swap(3, g8.at[heads_of(0)], g8.at[heads_of(PAIR)], PAIR)
    q_diag = swap(4, q8.at[heads_of(PAIR)], q8.at[heads_of(DIAG)], SIB)
    g_diag = swap(5, g8.at[heads_of(PAIR)], g8.at[heads_of(DIAG)], SIB)
    stats = [swap(5 + bits, stat, stat_in.at[bits - 1], bits) for bits in (PAIR, DIAG, SIB)]
    mid = swap(9, mid_out, mid_in, SIB)
    last = swap(10, last_out, last_in, PAIR)

    for load in loads[:2]:
        load.wait()
    pl.semaphore_wait(barrier, 2 * REACH + 3 + jnp.where(speaks, 5, 0))
    hops(0, "start")
    for load in loads[2:]:
        load.wait()
    for copy in (q_pair, q_sib, g_pair, g_sib):
        copy.start()

    @pl.when(speaks)
    def _():
        word(word_sem.at[0], speaker(1))
        word(word_sem.at[0], speaker(3))

    stat[0:8, :] = jnp.full((8, 256), HIDDEN, F32)
    stat[8:24, :] = jnp.zeros((16, 256), F32)
    rs_in[PLUS, half - 1, VAL] = jnp.zeros((PIECE, HEAD_DIM), BF16)
    rs_in[MINUS, half - 1, KEY] = jnp.zeros((PIECE, HEAD_DIM), BF16)

    def turn(bits):
        for h in range(2):
            at = slice(bits * 512 + h * 256, bits * 512 + (h + 1) * 256)
            q_t[:, at] = q8[at, :].T
            g_t[:, at] = g8[at, :].T

    lane = lax.broadcasted_iota(jnp.int32, (1, 256), 1)
    ahead = (
        lax.rem(lax.broadcasted_iota(jnp.int32, (2 * PIECE, 256), 0), PIECE)
        - lax.rem(lax.broadcasted_iota(jnp.int32, (2 * PIECE, 256), 1), SPAN)
        + core * PIECE
    )
    q_span0 = order_ref[2 * z]
    q_span1 = order_ref[2 * z + 1]

    def span_at(place):
        return pl.ds(place * SPAN if isinstance(place, int) else pl.multiple_of(place * SPAN, SPAN), SPAN)

    def reach_at(t):
        def reach_of(block):
            k_span = order_ref[2 * lax.rem(block, n_ctx) + chip]
            reach = jnp.where(lane < SPAN, (q_span0 - k_span) * SPAN, (q_span1 - k_span) * SPAN)
            return jnp.broadcast_to(reach, (PIECE, 256))

        return jnp.concatenate([reach_of(z + n_ctx - t), reach_of(z + t + half * (1 // (t + 1)))], axis=0)

    def forward(t, members, place):
        visible = ahead <= reach_at(t)
        key = jnp.concatenate([kv[t, 0, KEY], kv[t, 1, KEY]], axis=0)
        value = jnp.concatenate([kv[t, 0, VAL], kv[t, 1, VAL]], axis=0)
        for row in [2 * bits + h for bits in members for h in range(2)]:
            at = slice(row * 256, (row + 1) * 256)
            top_at, sum_at, dot_at = [slice(8 * i + row, 8 * i + row + 1) for i in range(3)]
            s = jnp.where(visible, dot(key, q_t[:, at]) * exponent_scale, HIDDEN)
            top = stat[top_at, :]
            new_top = jnp.maximum(top, jnp.max(s, axis=0, keepdims=True))
            p = jnp.exp2(s - new_top)
            dp = dot(value, g_t[:, at])
            shrink = jnp.exp2(top - new_top)
            stat[sum_at, :] = stat[sum_at, :] * shrink + jnp.sum(p, axis=0, keepdims=True)
            stat[dot_at, :] = stat[dot_at, :] * shrink + jnp.sum(p * dp, axis=0, keepdims=True)
            stat[top_at, :] = new_top
            m_blk[t, row : row + 1, :] = new_top
            p_buf[t, :, at] = p
            dp_buf[t, :, at] = dp
        if 0 in members:
            kv_t[KEY, :, span_at(place)] = key.T
            kv_t[VAL, :, span_at(place)] = value.T

    turn(0)
    q_sib.wait_recv()
    g_sib.wait_recv()
    turn(SIB)
    arrived(REACH)
    hops(REACH, "start")
    arrived(1)
    arrived(2)

    def near_pairs(t, carry):
        forward(t, (0, SIB), t)

        @pl.when(t == 1)
        def _():
            q_pair.wait_recv()
            q_diag.start()

        return carry

    def near_pairs_mate(t, carry):
        forward(t, (PAIR,), t)
        return carry

    def near_pairs_diag(t, carry):
        forward(t, (DIAG,), t)
        return carry

    far = (0, half - 1, half - 2)

    def far_bias():
        for i, t in enumerate(far):
            bias[span_at(i), :] = jnp.where(ahead <= reach_at(t), 0.0, HIDDEN)

    def far_pairs():
        def joined(kind):
            return jnp.concatenate([kv[t, side, kind] for t in far for side in range(2)], axis=0)

        key, value = joined(KEY), joined(VAL)
        for row in range(8):
            at = slice(row * 256, (row + 1) * 256)
            top_at, sum_at, dot_at = [slice(8 * i + row, 8 * i + row + 1) for i in range(3)]
            s = dot(key, q_t[:, at]) * exponent_scale + bias[...]
            top = stat[top_at, :]
            new_top = jnp.maximum(top, jnp.max(s, axis=0, keepdims=True))
            p = jnp.exp2(s - new_top)
            dp = dot(value, g_t[:, at])
            shrink = jnp.exp2(top - new_top)
            stat[sum_at, :] = stat[sum_at, :] * shrink + jnp.sum(p, axis=0, keepdims=True)
            stat[dot_at, :] = stat[dot_at, :] * shrink + jnp.sum(p * dp, axis=0, keepdims=True)
            stat[top_at, :] = new_top
            for i, t in enumerate(far):
                m_blk[t, row : row + 1, :] = new_top
                p_buf[t, :, at] = p[i * SPAN : (i + 1) * SPAN]
                dp_buf[t, :, at] = dp[i * SPAN : (i + 1) * SPAN]

    def far_turn():
        for t in far:
            for kind in (KEY, VAL):
                kv_t[kind, :, span_at(t)] = jnp.concatenate([kv[t, 0, kind], kv[t, 1, kind]], axis=0).T

    lax.fori_loop(1, REACH + 1, near_pairs, 0)

    @pl.when(speaks)
    def _():
        pl.semaphore_wait(word_sem.at[0], 2)
        word(word_sem.at[1], speaker(1))

    g_pair.wait_recv()
    g_diag.start()
    turn(PAIR)
    lax.fori_loop(1, REACH + 1, near_pairs_mate, 0)
    q_diag.wait_recv()
    g_diag.wait_recv()
    turn(DIAG)

    @pl.when(speaks)
    def _():
        pl.semaphore_wait(word_sem.at[1], 1)
        for step in range(1, 4):
            word(word_sem.at[2], lax.rem(column + step, 4) * 16 + place * 4 + member)

    lax.fori_loop(1, REACH + 1, near_pairs_diag, 0)
    far_bias()
    for t in range(REACH + 1, half + 1):
        arrived(t)
    far_pairs()

    for copy in stats:
        copy.start()
    far_turn()
    for copy in stats:
        copy.wait()

    def seen_by(bits, kind):
        if bits == 0:
            return stat[8 * kind : 8 * kind + 8, :]
        order = [8 * kind + 2 * (own ^ bits) for own in range(4)]
        return jnp.concatenate([stat_in[bits - 1, at : at + 2, :] for at in order], axis=0)

    tops = [seen_by(bits, 0) for bits in range(4)]
    top = jnp.maximum(jnp.maximum(tops[0], tops[1]), jnp.maximum(tops[2], tops[3]))
    weights = [jnp.exp2(one - top) for one in tops]
    total = sum(seen_by(bits, 1) * weights[bits] for bits in range(4))
    inverse = 1.0 / total
    both[0] = top
    both[1] = inverse
    both[2] = sum(seen_by(bits, 2) * weights[bits] for bits in range(4)) * inverse

    def grads_of(t):
        factor = jnp.exp2(m_blk[t] - both[0]) * both[1]
        row_dots = both[2]
        part = span_at(t)
        for row in range(8):
            at = slice(row * 256, (row + 1) * 256)
            p = p_buf[t, :, at] * factor[row : row + 1]
            pb[part, at] = p.astype(BF16)
            dsb[part, at] = (p * (dp_buf[t, :, at] - row_dots[row : row + 1])).astype(BF16)
        return dot(dsb[part, :], q8[...]) * score_scale, dot(pb[part, :], g8[...])

    def rows_of(bits):
        at = slice(bits * 512, (bits + 1) * 512)
        return dot(kv_t[VAL], pb[:, at]), dot(kv_t[KEY], dsb[:, at])

    def pass_on(direction, d):
        src, dst = rs_out.at[direction, d - 1], rs_in.at[direction, d - 1]
        if isinstance(d, int) and d == half:
            kind = KEY if direction == PLUS else VAL
            src, dst = src.at[kind], dst.at[kind]
        reach = (d - 1) % REACH + 1
        return remote(src, dst, rs_send.at[direction, d - 1], rs_recv.at[direction, d - 1], along(direction, reach), head)

    def side(direction):
        return slice(PIECE, 2 * PIECE) if direction == PLUS else slice(0, PIECE)

    grads = grads_of(0)
    for direction, kind in ((PLUS, KEY), (MINUS, VAL)):
        rs_out[direction, half - 1, kind] = grads[kind][PIECE:].astype(BF16)
        pass_on(direction, half).start()
    for kind in (KEY, VAL):
        own_grad[kind] = grads[kind][:PIECE]

    def reduce_step(i, carry):
        d = half - 1 - i - i // 2
        grads = grads_of(d)
        for direction in (PLUS, MINUS):
            for kind in (KEY, VAL):
                rs_out[direction, d - 1, kind] = grads[kind][side(direction)].astype(BF16)
            pass_on(direction, d).start()
        return carry

    lax.fori_loop(0, half - 2, reduce_step, 0)

    grads = grads_of(REACH)
    for kind in (KEY, VAL):
        near_grad[kind] = grads[kind]
    for i, bits in enumerate((SIB, DIAG)):
        for j, rows_sum in enumerate(rows_of(bits)):
            mid_out[i, j] = rows_sum.astype(BF16)
    mid.start()
    for i, bits in enumerate((0, PAIR)):
        o_t[i], dq_t[i] = rows_of(bits)
    for direction in (PLUS, MINUS):
        for d in range(REACH + 1, half + 1):
            pass_on(direction, d).wait_recv()
        for kind in (KEY, VAL):
            beyond = sum(rs_in[direction, d - 1, kind].astype(F32) for d in range(REACH + 1, half + 1))
            rs_out[direction, REACH - 1, kind] = (near_grad[kind, side(direction), :] + beyond).astype(BF16)
        pass_on(direction, REACH).start()

    mid.wait_recv()
    last_out[0] = (o_t[1] + mid_in[1, 0].astype(F32)).astype(BF16)
    last_out[1] = (dq_t[1] + mid_in[1, 1].astype(F32)).astype(BF16)
    last.start()

    @pl.when(jnp.logical_not(speaks))
    def _():
        pl.semaphore_wait(word_sem.at[2], 1)

    for direction in (PLUS, MINUS):
        for d in range(1, REACH + 1):
            pass_on(direction, d).wait_recv()
    for kind in (KEY, VAL):
        total = own_grad[kind]
        for direction in (PLUS, MINUS):
            for d in range(1, REACH + 1):
                total += rs_in[direction, d - 1, kind].astype(F32)
        for n in range(QUADS):
            f_out[n, 4 * kind : 4 * kind + 4, :] = total[4 * n : 4 * n + 4]

    def to_owner(n):
        return remote(f_out.at[n], f_in.at[quad], f_send.at[n], f_recv.at[0], z, member * 16 + n)

    row_of_chips = lax.rem(head, 16) // 2
    places = [(away, other) for away in (4, 3, 5, 2, 6, 1, 7, 0) for other in range(2)]

    def owner(away, other):
        return 2 * lax.rem(row_of_chips + away, 8) + other

    for away, other in places:
        n = owner(away, other)
        if away:
            to_owner(n).start()
        else:
            here = head == member * 16 + n

            @pl.when(here)
            def _():
                pltpu.make_async_copy(f_out.at[n], f_in.at[quad], f_recv.at[0]).start()

            @pl.when(jnp.logical_not(here))
            def _():
                to_owner(n).start()

    last.wait_recv()
    for h in range(2):
        at = slice(h * 256, (h + 1) * 256)
        cols_h = slice(h * HEAD_DIM, (h + 1) * HEAD_DIM)
        for i, part, out, scale in ((0, o_t, rows_ref.at[0], 1.0), (1, dq_t, rows_ref.at[1], score_scale)):
            rows_sum = part[0, :, at] + mid_in[0, i, :, at].astype(F32) + last_in[i, :, at].astype(F32)
            out[:, cols_h] = (rows_sum * scale).T.astype(BF16)

    for copy in (q_sib, g_sib, q_pair, g_pair, q_diag, g_diag, mid, last):
        copy.wait_send()
    for source in range(0, half, REACH):
        hops(source, "wait_send")
    for direction in (PLUS, MINUS):
        for d in range(1, half + 1):
            pass_on(direction, d).wait_send()
    for away, other in places:
        n = owner(away, other)
        if away:
            to_owner(n).wait_send()
        else:

            @pl.when(head != member * 16 + n)
            def _():
                to_owner(n).wait_send()

    pltpu.make_async_copy(f_out, f_in, f_recv.at[0]).wait()
    for g in range(QUADS // 2):
        at = slice(g * HEAD_DIM, (g + 1) * HEAD_DIM)
        summed = f_in[2 * g] + f_in[2 * g + 1]
        grads_ref[:, at] = summed.astype(BF16)


def per_device(query_rows, key_rows, value_rows, out_grad, span_order):
    n_ctx = lax.axis_size("ctx")
    half = n_ctx // 2
    vmem = pltpu.VMEM
    dma = pltpu.SemaphoreType.DMA
    outside = pl.BlockSpec(memory_space=pltpu.HBM)
    local = pl.BlockSpec(memory_space=pltpu.VMEM)
    rows, grads = pl.pallas_call(
        functools.partial(attention_kernel, n_ctx),
        out_shape=(
            jax.ShapeDtypeStruct((2, 256, 256), BF16),
            jax.ShapeDtypeStruct((8, 1024), BF16),
        ),
        in_specs=[pl.BlockSpec(memory_space=pltpu.SMEM), outside, outside, outside, outside],
        out_specs=(local, local),
        scratch_shapes=[
            vmem((2048, 128), BF16),
            vmem((2048, 128), BF16),
            vmem((128, 2048), BF16),
            vmem((128, 2048), BF16),
            vmem((3 * SPAN, 256), F32),
            vmem((half, 2, 2, PIECE, 128), BF16),
            vmem((2, 128, half * 128), BF16),
            vmem((half, 128, 2048), F32),
            vmem((half, 128, 2048), F32),
            vmem((half, 8, 256), F32),
            vmem((24, 256), F32),
            vmem((3, 24, 256), F32),
            vmem((3, 8, 256), F32),
            vmem((half * 128, 2048), BF16),
            vmem((half * 128, 2048), BF16),
            vmem((2, 128, 512), F32),
            vmem((2, 128, 512), F32),
            vmem((2, 2, 128, 512), BF16),
            vmem((2, 2, 128, 512), BF16),
            vmem((2, 128, 512), BF16),
            vmem((2, 128, 512), BF16),
            vmem((2, PIECE, 128), F32),
            vmem((2, 2 * PIECE, 128), F32),
            vmem((2, half, 2, PIECE, 128), BF16),
            vmem((2, half, 2, PIECE, 128), BF16),
            vmem((QUADS, 8, 128), F32),
            vmem((QUADS, 8, 128), F32),
            dma((6,)),
            dma((11,)),
            dma((11,)),
            dma((2, half)),
            dma((2, half)),
            dma((2, half)),
            dma((2, half)),
            dma((QUADS,)),
            dma((1,)),
            pltpu.SemaphoreType.REGULAR((3,)),
        ],
        compiler_params=pltpu.CompilerParams(
            collective_id=0, has_side_effects=True, vmem_limit_bytes=62 * 1024 * 1024
        ),
    )(span_order, query_rows, key_rows, value_rows, out_grad)
    return rows[0], rows[1], grads[:4], grads[4:]


def solution(mesh):
    in_specs = (P("ctx", "head"), P("ctx", None), P("ctx", None), P("ctx", "head"), P())
    out_specs = (
        P("ctx", "head"),
        P("ctx", "head"),
        P(("ctx", "head"), None),
        P(("ctx", "head"), None),
    )
    return jax.shard_map(
        per_device, mesh=mesh, in_specs=in_specs, out_specs=out_specs, check_vma=False
    )
```

```python
import functools
import math

import jax
import jax.numpy as jnp
from jax import lax
from jax.experimental import pallas as pl
from jax.experimental.pallas import tpu as pltpu
from jax.sharding import PartitionSpec as P

HEAD_DIM = 128
SPAN = 128
PIECE = 64
QUADS = 16
HIDDEN = -1e30
F32 = jnp.float32
BF16 = jnp.bfloat16
MESH = pl.DeviceIdType.MESH
PLUS, MINUS = 0, 1
KEY, VAL = 0, 1
SIB, PAIR, DIAG = 1, 2, 3
REACH = 3


def dot(a, b):
    return jnp.dot(a, b, preferred_element_type=F32)


def attention_kernel(
    n_ctx,
    order_ref,
    q_hbm,
    k_hbm,
    v_hbm,
    g_hbm,
    rows_ref,
    grads_ref,
    q8,
    g8,
    q_t,
    g_t,
    bias,
    kv,
    kv_t,
    p_buf,
    dp_buf,
    m_blk,
    stat,
    stat_in,
    both,
    pb,
    dsb,
    o_t,
    dq_t,
    mid_out,
    mid_in,
    last_out,
    last_in,
    own_grad,
    near_grad,
    rs_in,
    rs_out,
    f_out,
    f_in,
    load_sem,
    swap_send,
    swap_recv,
    kv_send,
    kv_recv,
    rs_send,
    rs_recv,
    f_send,
    f_recv,
    word_sem,
):
    half = n_ctx // 2
    z = lax.axis_index("ctx")
    head = lax.axis_index("head")
    group = head // 8
    quad = head // 4
    member = head % 4
    core = head % 2
    chip = member // 2
    sibling = head + 1 - 2 * core
    score_scale = 1.0 / math.sqrt(HEAD_DIM)
    exponent_scale = score_scale * math.log2(math.e)

    def mate(bits):
        other = head
        if bits & SIB:
            other = other + 1 - 2 * core
        if bits & PAIR:
            other = other + 2 - 4 * chip
        return other

    def along(direction, reach):
        return lax.rem(z + (reach if direction == PLUS else n_ctx - reach), n_ctx)

    rows = pl.ds(pl.multiple_of(member * PIECE, PIECE), PIECE)
    cols = pl.ds(pl.multiple_of(group * HEAD_DIM, HEAD_DIM), HEAD_DIM)
    loads = [
        pltpu.make_async_copy(k_hbm.at[rows, cols], kv.at[0, 0, KEY], load_sem.at[0]),
        pltpu.make_async_copy(v_hbm.at[rows, cols], kv.at[0, 0, VAL], load_sem.at[1]),
    ]
    for h in range(2):
        part = pl.ds(h * HEAD_DIM, HEAD_DIM)
        loads.append(pltpu.make_async_copy(q_hbm.at[:, part], q8.at[pl.ds(h * 256, 256)], load_sem.at[2 + h]))
        loads.append(pltpu.make_async_copy(g_hbm.at[:, part], g8.at[pl.ds(h * 256, 256)], load_sem.at[4 + h]))
    for load in loads:
        load.start()

    barrier = pltpu.get_barrier_semaphore()

    def greet(ctx_id, head_id):
        pl.semaphore_signal(barrier, inc=1, device_id=(ctx_id, head_id), device_id_type=MESH)

    for reach in range(REACH, 0, -1):
        for direction in (PLUS, MINUS):
            greet(along(direction, reach), head)
    for bits in (SIB, PAIR, DIAG):
        greet(z, mate(bits))
    column = head // 16
    place = quad % 4
    speaks = column == member

    def speaker(step):
        return column * 16 + lax.rem(place + step, 4) * 4 + member

    @pl.when(speaks)
    def _():
        greet(z, speaker(1))
        greet(z, speaker(3))

    @pl.when(jnp.logical_not(speaks))
    def _():
        greet(z, member * 16 + place * 4 + member)

    def word(sem, head_id):
        pl.semaphore_signal(sem, inc=1, device_id=(z, head_id), device_id_type=MESH)

    def remote(src, dst, send, recv, ctx_id, head_id):
        return pltpu.make_async_remote_copy(
            src_ref=src,
            dst_ref=dst,
            send_sem=send,
            recv_sem=recv,
            device_id=(ctx_id, head_id),
            device_id_type=MESH,
        )

    def hop(direction, source, reach):
        t = source + reach
        src = kv.at[source, direction if source else 0]
        dst = kv.at[t % half, direction if t < half else 1]
        if t == half:
            kind = KEY if direction == PLUS else VAL
            src, dst = src.at[kind], dst.at[kind]
        return remote(src, dst, kv_send.at[direction, t - 1], kv_recv.at[direction, t - 1], along(direction, reach), head)

    def hops(source, action):
        for reach in range(REACH, 0, -1):
            for direction in (PLUS, MINUS):
                getattr(hop(direction, source, reach), action)()

    def arrived(t):
        for direction in (PLUS, MINUS):
            hop(direction, (t - 1) // REACH * REACH, 1 + (t - 1) % REACH).wait_recv()

    def swap(i, src, dst, bits):
        return remote(src, dst, swap_send.at[i], swap_recv.at[i], z, mate(bits))

    def heads_of(bits):
        return pl.ds(bits * 512, 512)

    q_sib = swap(0, q8.at[heads_of(0)], q8.at[heads_of(SIB)], SIB)
    g_sib = swap(1, g8.at[heads_of(0)], g8.at[heads_of(SIB)], SIB)
    q_pair = swap(2, q8.at[heads_of(0)], q8.at[heads_of(PAIR)], PAIR)
    g_pair = swap(3, g8.at[heads_of(0)], g8.at[heads_of(PAIR)], PAIR)
    q_diag = swap(4, q8.at[heads_of(PAIR)], q8.at[heads_of(DIAG)], SIB)
    g_diag = swap(5, g8.at[heads_of(PAIR)], g8.at[heads_of(DIAG)], SIB)
    stats = [swap(5 + bits, stat, stat_in.at[bits - 1], bits) for bits in (PAIR, DIAG, SIB)]
    mid = swap(9, mid_out, mid_in, SIB)
    last = swap(10, last_out, last_in, PAIR)

    for load in loads[:2]:
        load.wait()
    pl.semaphore_wait(barrier, 2 * REACH + 3 + jnp.where(speaks, 5, 0))
    hops(0, "start")
    for load in loads[2:]:
        load.wait()
    for copy in (q_pair, q_sib, g_pair, g_sib):
        copy.start()

    @pl.when(speaks)
    def _():
        word(word_sem.at[0], speaker(1))
        word(word_sem.at[0], speaker(3))

    stat[0:8, :] = jnp.full((8, 256), HIDDEN, F32)
    stat[8:24, :] = jnp.zeros((16, 256), F32)
    rs_in[PLUS, half - 1, VAL] = jnp.zeros((PIECE, HEAD_DIM), BF16)
    rs_in[MINUS, half - 1, KEY] = jnp.zeros((PIECE, HEAD_DIM), BF16)

    def turn(bits):
        for h in range(2):
            at = slice(bits * 512 + h * 256, bits * 512 + (h + 1) * 256)
            q_t[:, at] = q8[at, :].T
            g_t[:, at] = g8[at, :].T

    lane = lax.broadcasted_iota(jnp.int32, (1, 256), 1)
    ahead = (
        lax.rem(lax.broadcasted_iota(jnp.int32, (2 * PIECE, 256), 0), PIECE)
        - lax.rem(lax.broadcasted_iota(jnp.int32, (2 * PIECE, 256), 1), SPAN)
        + core * PIECE
    )
    q_span0 = order_ref[2 * z]
    q_span1 = order_ref[2 * z + 1]

    def span_at(place):
        return pl.ds(place * SPAN if isinstance(place, int) else pl.multiple_of(place * SPAN, SPAN), SPAN)

    def reach_at(t):
        def reach_of(block):
            k_span = order_ref[2 * lax.rem(block, n_ctx) + chip]
            reach = jnp.where(lane < SPAN, (q_span0 - k_span) * SPAN, (q_span1 - k_span) * SPAN)
            return jnp.broadcast_to(reach, (PIECE, 256))

        return jnp.concatenate([reach_of(z + n_ctx - t), reach_of(z + t + half * (1 // (t + 1)))], axis=0)

    def forward(t, members, place):
        visible = ahead <= reach_at(t)
        key = jnp.concatenate([kv[t, 0, KEY], kv[t, 1, KEY]], axis=0)
        value = jnp.concatenate([kv[t, 0, VAL], kv[t, 1, VAL]], axis=0)
        for row in [2 * bits + h for bits in members for h in range(2)]:
            at = slice(row * 256, (row + 1) * 256)
            top_at, sum_at, dot_at = [slice(8 * i + row, 8 * i + row + 1) for i in range(3)]
            s = jnp.where(visible, dot(key, q_t[:, at]) * exponent_scale, HIDDEN)
            top = stat[top_at, :]
            new_top = jnp.maximum(top, jnp.max(s, axis=0, keepdims=True))
            p = jnp.exp2(s - new_top)
            dp = dot(value, g_t[:, at])
            shrink = jnp.exp2(top - new_top)
            stat[sum_at, :] = stat[sum_at, :] * shrink + jnp.sum(p, axis=0, keepdims=True)
            stat[dot_at, :] = stat[dot_at, :] * shrink + jnp.sum(p * dp, axis=0, keepdims=True)
            stat[top_at, :] = new_top
            m_blk[t, row : row + 1, :] = new_top
            p_buf[t, :, at] = p
            dp_buf[t, :, at] = dp
        if 0 in members:
            kv_t[KEY, :, span_at(place)] = key.T
            kv_t[VAL, :, span_at(place)] = value.T

    turn(0)
    q_sib.wait_recv()
    g_sib.wait_recv()
    turn(SIB)
    arrived(REACH)
    hops(REACH, "start")
    arrived(1)
    arrived(2)

    def near_pairs(t, carry):
        forward(t, (0, SIB), t)

        @pl.when(t == 1)
        def _():
            q_pair.wait_recv()
            q_diag.start()

        return carry

    def near_pairs_mate(t, carry):
        forward(t, (PAIR,), t)
        return carry

    def near_pairs_diag(t, carry):
        forward(t, (DIAG,), t)
        return carry

    far = (0, half - 1, half - 2)

    def far_bias():
        for i, t in enumerate(far):
            bias[span_at(i), :] = jnp.where(ahead <= reach_at(t), 0.0, HIDDEN)

    def far_pairs():
        def joined(kind):
            return jnp.concatenate([kv[t, side, kind] for t in far for side in range(2)], axis=0)

        key, value = joined(KEY), joined(VAL)
        for row in range(8):
            at = slice(row * 256, (row + 1) * 256)
            top_at, sum_at, dot_at = [slice(8 * i + row, 8 * i + row + 1) for i in range(3)]
            s = dot(key, q_t[:, at]) * exponent_scale + bias[...]
            top = stat[top_at, :]
            new_top = jnp.maximum(top, jnp.max(s, axis=0, keepdims=True))
            p = jnp.exp2(s - new_top)
            dp = dot(value, g_t[:, at])
            shrink = jnp.exp2(top - new_top)
            stat[sum_at, :] = stat[sum_at, :] * shrink + jnp.sum(p, axis=0, keepdims=True)
            stat[dot_at, :] = stat[dot_at, :] * shrink + jnp.sum(p * dp, axis=0, keepdims=True)
            stat[top_at, :] = new_top
            for i, t in enumerate(far):
                m_blk[t, row : row + 1, :] = new_top
                p_buf[t, :, at] = p[i * SPAN : (i + 1) * SPAN]
                dp_buf[t, :, at] = dp[i * SPAN : (i + 1) * SPAN]

    def far_turn():
        for t in far:
            for kind in (KEY, VAL):
                kv_t[kind, :, span_at(t)] = jnp.concatenate([kv[t, 0, kind], kv[t, 1, kind]], axis=0).T

    lax.fori_loop(1, REACH + 1, near_pairs, 0)

    @pl.when(speaks)
    def _():
        pl.semaphore_wait(word_sem.at[0], 2)
        word(word_sem.at[1], speaker(1))

    g_pair.wait_recv()
    g_diag.start()
    turn(PAIR)
    lax.fori_loop(1, REACH + 1, near_pairs_mate, 0)
    q_diag.wait_recv()
    g_diag.wait_recv()
    turn(DIAG)

    @pl.when(speaks)
    def _():
        pl.semaphore_wait(word_sem.at[1], 1)
        for step in range(1, 4):
            word(word_sem.at[2], lax.rem(column + step, 4) * 16 + place * 4 + member)

    lax.fori_loop(1, REACH + 1, near_pairs_diag, 0)
    far_bias()
    for t in range(REACH + 1, half + 1):
        arrived(t)
    far_pairs()

    for copy in stats:
        copy.start()
    far_turn()
    for copy in stats:
        copy.wait()

    def seen_by(bits, kind):
        if bits == 0:
            return stat[8 * kind : 8 * kind + 8, :]
        order = [8 * kind + 2 * (own ^ bits) for own in range(4)]
        return jnp.concatenate([stat_in[bits - 1, at : at + 2, :] for at in order], axis=0)

    tops = [seen_by(bits, 0) for bits in range(4)]
    top = jnp.maximum(jnp.maximum(tops[0], tops[1]), jnp.maximum(tops[2], tops[3]))
    weights = [jnp.exp2(one - top) for one in tops]
    total = sum(seen_by(bits, 1) * weights[bits] for bits in range(4))
    inverse = 1.0 / total
    both[0] = top
    both[1] = inverse
    both[2] = sum(seen_by(bits, 2) * weights[bits] for bits in range(4)) * inverse

    def grads_of(t):
        factor = jnp.exp2(m_blk[t] - both[0]) * both[1]
        row_dots = both[2]
        part = span_at(t)
        for row in range(8):
            at = slice(row * 256, (row + 1) * 256)
            p = p_buf[t, :, at] * factor[row : row + 1]
            pb[part, at] = p.astype(BF16)
            dsb[part, at] = (p * (dp_buf[t, :, at] - row_dots[row : row + 1])).astype(BF16)
        return dot(dsb[part, :], q8[...]) * score_scale, dot(pb[part, :], g8[...])

    def rows_of(bits):
        at = slice(bits * 512, (bits + 1) * 512)
        return dot(kv_t[VAL], pb[:, at]), dot(kv_t[KEY], dsb[:, at])

    def pass_on(direction, d):
        src, dst = rs_out.at[direction, d - 1], rs_in.at[direction, d - 1]
        if isinstance(d, int) and d == half:
            kind = KEY if direction == PLUS else VAL
            src, dst = src.at[kind], dst.at[kind]
        reach = (d - 1) % REACH + 1
        return remote(src, dst, rs_send.at[direction, d - 1], rs_recv.at[direction, d - 1], along(direction, reach), head)

    def side(direction):
        return slice(PIECE, 2 * PIECE) if direction == PLUS else slice(0, PIECE)

    grads = grads_of(0)
    for direction, kind in ((PLUS, KEY), (MINUS, VAL)):
        rs_out[direction, half - 1, kind] = grads[kind][PIECE:].astype(BF16)
        pass_on(direction, half).start()
    for kind in (KEY, VAL):
        own_grad[kind] = grads[kind][:PIECE]

    def reduce_step(i, carry):
        d = half - 1 - i - i // 2
        grads = grads_of(d)
        for direction in (PLUS, MINUS):
            for kind in (KEY, VAL):
                rs_out[direction, d - 1, kind] = grads[kind][side(direction)].astype(BF16)
            pass_on(direction, d).start()
        return carry

    lax.fori_loop(0, half - 2, reduce_step, 0)

    grads = grads_of(REACH)
    for kind in (KEY, VAL):
        near_grad[kind] = grads[kind]
    for i, bits in enumerate((SIB, DIAG)):
        for j, rows_sum in enumerate(rows_of(bits)):
            mid_out[i, j] = rows_sum.astype(BF16)
    mid.start()
    for direction in (PLUS, MINUS):
        for d in range(REACH + 1, half + 1):
            pass_on(direction, d).wait_recv()
        for kind in (KEY, VAL):
            beyond = sum(rs_in[direction, d - 1, kind].astype(F32) for d in range(REACH + 1, half + 1))
            rs_out[direction, REACH - 1, kind] = (near_grad[kind, side(direction), :] + beyond).astype(BF16)
        pass_on(direction, REACH).start()

    for i, bits in enumerate((0, PAIR)):
        o_t[i], dq_t[i] = rows_of(bits)
    mid.wait_recv()
    last_out[0] = (o_t[1] + mid_in[1, 0].astype(F32)).astype(BF16)
    last_out[1] = (dq_t[1] + mid_in[1, 1].astype(F32)).astype(BF16)
    last.start()

    @pl.when(jnp.logical_not(speaks))
    def _():
        pl.semaphore_wait(word_sem.at[2], 1)

    for direction in (PLUS, MINUS):
        for d in range(1, REACH + 1):
            pass_on(direction, d).wait_recv()
    for kind in (KEY, VAL):
        total = own_grad[kind]
        for direction in (PLUS, MINUS):
            for d in range(1, REACH + 1):
                total += rs_in[direction, d - 1, kind].astype(F32)
        for n in range(QUADS):
            f_out[n, 4 * kind : 4 * kind + 4, :] = total[4 * n : 4 * n + 4]

    def to_owner(n):
        return remote(f_out.at[n], f_in.at[quad], f_send.at[n], f_recv.at[0], z, member * 16 + n)

    row_of_chips = lax.rem(head, 16) // 2
    places = [(away, other) for away in (4, 3, 5, 2, 6, 1, 7, 0) for other in range(2)]

    def owner(away, other):
        return 2 * lax.rem(row_of_chips + away, 8) + other

    for away, other in places:
        n = owner(away, other)
        if away:
            to_owner(n).start()
        else:
            here = head == member * 16 + n

            @pl.when(here)
            def _():
                pltpu.make_async_copy(f_out.at[n], f_in.at[quad], f_recv.at[0]).start()

            @pl.when(jnp.logical_not(here))
            def _():
                to_owner(n).start()

    last.wait_recv()
    for h in range(2):
        at = slice(h * 256, (h + 1) * 256)
        cols_h = slice(h * HEAD_DIM, (h + 1) * HEAD_DIM)
        for i, part, out, scale in ((0, o_t, rows_ref.at[0], 1.0), (1, dq_t, rows_ref.at[1], score_scale)):
            rows_sum = part[0, :, at] + mid_in[0, i, :, at].astype(F32) + last_in[i, :, at].astype(F32)
            out[:, cols_h] = (rows_sum * scale).T.astype(BF16)

    for copy in (q_sib, g_sib, q_pair, g_pair, q_diag, g_diag, mid, last):
        copy.wait_send()
    for source in range(0, half, REACH):
        hops(source, "wait_send")
    for direction in (PLUS, MINUS):
        for d in range(1, half + 1):
            pass_on(direction, d).wait_send()
    for away, other in places:
        n = owner(away, other)
        if away:
            to_owner(n).wait_send()
        else:

            @pl.when(head != member * 16 + n)
            def _():
                to_owner(n).wait_send()

    pltpu.make_async_copy(f_out, f_in, f_recv.at[0]).wait()
    for g in range(QUADS // 2):
        at = slice(g * HEAD_DIM, (g + 1) * HEAD_DIM)
        summed = f_in[2 * g] + f_in[2 * g + 1]
        grads_ref[:, at] = summed.astype(BF16)


def per_device(query_rows, key_rows, value_rows, out_grad, span_order):
    n_ctx = lax.axis_size("ctx")
    half = n_ctx // 2
    vmem = pltpu.VMEM
    dma = pltpu.SemaphoreType.DMA
    outside = pl.BlockSpec(memory_space=pltpu.HBM)
    local = pl.BlockSpec(memory_space=pltpu.VMEM)
    rows, grads = pl.pallas_call(
        functools.partial(attention_kernel, n_ctx),
        out_shape=(
            jax.ShapeDtypeStruct((2, 256, 256), BF16),
            jax.ShapeDtypeStruct((8, 1024), BF16),
        ),
        in_specs=[pl.BlockSpec(memory_space=pltpu.SMEM), outside, outside, outside, outside],
        out_specs=(local, local),
        scratch_shapes=[
            vmem((2048, 128), BF16),
            vmem((2048, 128), BF16),
            vmem((128, 2048), BF16),
            vmem((128, 2048), BF16),
            vmem((3 * SPAN, 256), F32),
            vmem((half, 2, 2, PIECE, 128), BF16),
            vmem((2, 128, half * 128), BF16),
            vmem((half, 128, 2048), F32),
            vmem((half, 128, 2048), F32),
            vmem((half, 8, 256), F32),
            vmem((24, 256), F32),
            vmem((3, 24, 256), F32),
            vmem((3, 8, 256), F32),
            vmem((half * 128, 2048), BF16),
            vmem((half * 128, 2048), BF16),
            vmem((2, 128, 512), F32),
            vmem((2, 128, 512), F32),
            vmem((2, 2, 128, 512), BF16),
            vmem((2, 2, 128, 512), BF16),
            vmem((2, 128, 512), BF16),
            vmem((2, 128, 512), BF16),
            vmem((2, PIECE, 128), F32),
            vmem((2, 2 * PIECE, 128), F32),
            vmem((2, half, 2, PIECE, 128), BF16),
            vmem((2, half, 2, PIECE, 128), BF16),
            vmem((QUADS, 8, 128), F32),
            vmem((QUADS, 8, 128), F32),
            dma((6,)),
            dma((11,)),
            dma((11,)),
            dma((2, half)),
            dma((2, half)),
            dma((2, half)),
            dma((2, half)),
            dma((QUADS,)),
            dma((1,)),
            pltpu.SemaphoreType.REGULAR((3,)),
        ],
        compiler_params=pltpu.CompilerParams(
            collective_id=0, has_side_effects=True, vmem_limit_bytes=62 * 1024 * 1024
        ),
    )(span_order, query_rows, key_rows, value_rows, out_grad)
    return rows[0], rows[1], grads[:4], grads[4:]


def solution(mesh):
    in_specs = (P("ctx", "head"), P("ctx", None), P("ctx", None), P("ctx", "head"), P())
    out_specs = (
        P("ctx", "head"),
        P("ctx", "head"),
        P(("ctx", "head"), None),
        P(("ctx", "head"), None),
    )
    return jax.shard_map(
        per_device, mesh=mesh, in_specs=in_specs, out_specs=out_specs, check_vma=False
    )
```

```python
import functools
import math

import jax
import jax.numpy as jnp
from jax import lax
from jax.experimental import pallas as pl
from jax.experimental.pallas import tpu as pltpu
from jax.sharding import PartitionSpec as P

HEAD_DIM = 128
SPAN = 128
PIECE = 64
QUADS = 16
HIDDEN = -1e30
F32 = jnp.float32
BF16 = jnp.bfloat16
MESH = pl.DeviceIdType.MESH
PLUS, MINUS = 0, 1
KEY, VAL = 0, 1
SIB, PAIR, DIAG = 1, 2, 3
REACH = 3


def dot(a, b):
    return jnp.dot(a, b, preferred_element_type=F32)


def attention_kernel(
    n_ctx,
    order_ref,
    q_hbm,
    k_hbm,
    v_hbm,
    g_hbm,
    rows_ref,
    grads_ref,
    q8,
    g8,
    q_t,
    g_t,
    bias,
    kv,
    kv_t,
    p_buf,
    dp_buf,
    m_blk,
    stat,
    stat_in,
    both,
    pb,
    dsb,
    o_t,
    dq_t,
    mid_out,
    mid_in,
    last_out,
    last_in,
    own_grad,
    near_grad,
    rs_in,
    rs_out,
    f_out,
    f_in,
    load_sem,
    swap_send,
    swap_recv,
    kv_send,
    kv_recv,
    rs_send,
    rs_recv,
    f_send,
    f_recv,
    word_sem,
):
    half = n_ctx // 2
    z = lax.axis_index("ctx")
    head = lax.axis_index("head")
    group = head // 8
    quad = head // 4
    member = head % 4
    core = head % 2
    chip = member // 2
    sibling = head + 1 - 2 * core
    score_scale = 1.0 / math.sqrt(HEAD_DIM)
    exponent_scale = score_scale * math.log2(math.e)

    def mate(bits):
        other = head
        if bits & SIB:
            other = other + 1 - 2 * core
        if bits & PAIR:
            other = other + 2 - 4 * chip
        return other

    def along(direction, reach):
        return lax.rem(z + (reach if direction == PLUS else n_ctx - reach), n_ctx)

    rows = pl.ds(pl.multiple_of(member * PIECE, PIECE), PIECE)
    cols = pl.ds(pl.multiple_of(group * HEAD_DIM, HEAD_DIM), HEAD_DIM)
    loads = [
        pltpu.make_async_copy(k_hbm.at[rows, cols], kv.at[0, 0, KEY], load_sem.at[0]),
        pltpu.make_async_copy(v_hbm.at[rows, cols], kv.at[0, 0, VAL], load_sem.at[1]),
    ]
    for h in range(2):
        part = pl.ds(h * HEAD_DIM, HEAD_DIM)
        loads.append(pltpu.make_async_copy(q_hbm.at[:, part], q8.at[pl.ds(h * 256, 256)], load_sem.at[2 + h]))
        loads.append(pltpu.make_async_copy(g_hbm.at[:, part], g8.at[pl.ds(h * 256, 256)], load_sem.at[4 + h]))
    for load in loads:
        load.start()

    barrier = pltpu.get_barrier_semaphore()

    def greet(ctx_id, head_id):
        pl.semaphore_signal(barrier, inc=1, device_id=(ctx_id, head_id), device_id_type=MESH)

    for reach in range(REACH, 0, -1):
        for direction in (PLUS, MINUS):
            greet(along(direction, reach), head)
    for bits in (SIB, PAIR, DIAG):
        greet(z, mate(bits))
    column = head // 16
    place = quad % 4
    speaks = column == member

    def speaker(step):
        return column * 16 + lax.rem(place + step, 4) * 4 + member

    @pl.when(speaks)
    def _():
        greet(z, speaker(1))
        greet(z, speaker(3))

    @pl.when(jnp.logical_not(speaks))
    def _():
        greet(z, member * 16 + place * 4 + member)

    def word(sem, head_id):
        pl.semaphore_signal(sem, inc=1, device_id=(z, head_id), device_id_type=MESH)

    def remote(src, dst, send, recv, ctx_id, head_id):
        return pltpu.make_async_remote_copy(
            src_ref=src,
            dst_ref=dst,
            send_sem=send,
            recv_sem=recv,
            device_id=(ctx_id, head_id),
            device_id_type=MESH,
        )

    def hop(direction, source, reach):
        t = source + reach
        src = kv.at[source, direction if source else 0]
        dst = kv.at[t % half, direction if t < half else 1]
        if t == half:
            kind = KEY if direction == PLUS else VAL
            src, dst = src.at[kind], dst.at[kind]
        return remote(src, dst, kv_send.at[direction, t - 1], kv_recv.at[direction, t - 1], along(direction, reach), head)

    def hops(source, action):
        for reach in range(REACH, 0, -1):
            for direction in (PLUS, MINUS):
                getattr(hop(direction, source, reach), action)()

    def arrived(t):
        for direction in (PLUS, MINUS):
            hop(direction, (t - 1) // REACH * REACH, 1 + (t - 1) % REACH).wait_recv()

    def swap(i, src, dst, bits):
        return remote(src, dst, swap_send.at[i], swap_recv.at[i], z, mate(bits))

    def heads_of(bits):
        return pl.ds(bits * 512, 512)

    q_sib = swap(0, q8.at[heads_of(0)], q8.at[heads_of(SIB)], SIB)
    g_sib = swap(1, g8.at[heads_of(0)], g8.at[heads_of(SIB)], SIB)
    q_pair = swap(2, q8.at[heads_of(0)], q8.at[heads_of(PAIR)], PAIR)
    g_pair = swap(3, g8.at[heads_of(0)], g8.at[heads_of(PAIR)], PAIR)
    q_diag = swap(4, q8.at[heads_of(PAIR)], q8.at[heads_of(DIAG)], SIB)
    g_diag = swap(5, g8.at[heads_of(PAIR)], g8.at[heads_of(DIAG)], SIB)
    stats = [swap(5 + bits, stat, stat_in.at[bits - 1], bits) for bits in (PAIR, DIAG, SIB)]
    mid = swap(9, mid_out, mid_in, SIB)
    last = swap(10, last_out, last_in, PAIR)

    for load in loads[:2]:
        load.wait()
    pl.semaphore_wait(barrier, 2 * REACH + 3 + jnp.where(speaks, 5, 0))
    hops(0, "start")
    for load in loads[2:]:
        load.wait()
    for copy in (q_pair, q_sib, g_pair, g_sib):
        copy.start()

    @pl.when(speaks)
    def _():
        word(word_sem.at[0], speaker(1))
        word(word_sem.at[0], speaker(3))

    stat[0:8, :] = jnp.full((8, 256), HIDDEN, F32)
    stat[8:24, :] = jnp.zeros((16, 256), F32)
    rs_in[PLUS, half - 1, VAL] = jnp.zeros((PIECE, HEAD_DIM), BF16)
    rs_in[MINUS, half - 1, KEY] = jnp.zeros((PIECE, HEAD_DIM), BF16)

    def turn(bits):
        for h in range(2):
            at = slice(bits * 512 + h * 256, bits * 512 + (h + 1) * 256)
            q_t[:, at] = q8[at, :].T
            g_t[:, at] = g8[at, :].T

    lane = lax.broadcasted_iota(jnp.int32, (1, 256), 1)
    ahead = (
        lax.rem(lax.broadcasted_iota(jnp.int32, (2 * PIECE, 256), 0), PIECE)
        - lax.rem(lax.broadcasted_iota(jnp.int32, (2 * PIECE, 256), 1), SPAN)
        + core * PIECE
    )
    q_span0 = order_ref[2 * z]
    q_span1 = order_ref[2 * z + 1]

    def span_at(place):
        return pl.ds(place * SPAN if isinstance(place, int) else pl.multiple_of(place * SPAN, SPAN), SPAN)

    def reach_at(t):
        def reach_of(block):
            k_span = order_ref[2 * lax.rem(block, n_ctx) + chip]
            reach = jnp.where(lane < SPAN, (q_span0 - k_span) * SPAN, (q_span1 - k_span) * SPAN)
            return jnp.broadcast_to(reach, (PIECE, 256))

        return jnp.concatenate([reach_of(z + n_ctx - t), reach_of(z + t + half * (1 // (t + 1)))], axis=0)

    def forward(t, members, place):
        visible = ahead <= reach_at(t)
        key = jnp.concatenate([kv[t, 0, KEY], kv[t, 1, KEY]], axis=0)
        value = jnp.concatenate([kv[t, 0, VAL], kv[t, 1, VAL]], axis=0)
        for row in [2 * bits + h for bits in members for h in range(2)]:
            at = slice(row * 256, (row + 1) * 256)
            top_at, sum_at, dot_at = [slice(8 * i + row, 8 * i + row + 1) for i in range(3)]
            s = jnp.where(visible, dot(key, q_t[:, at]) * exponent_scale, HIDDEN)
            top = stat[top_at, :]
            new_top = jnp.maximum(top, jnp.max(s, axis=0, keepdims=True))
            p = jnp.exp2(s - new_top)
            dp = dot(value, g_t[:, at])
            shrink = jnp.exp2(top - new_top)
            stat[sum_at, :] = stat[sum_at, :] * shrink + jnp.sum(p, axis=0, keepdims=True)
            stat[dot_at, :] = stat[dot_at, :] * shrink + jnp.sum(p * dp, axis=0, keepdims=True)
            stat[top_at, :] = new_top
            m_blk[t, row : row + 1, :] = new_top
            p_buf[t, :, at] = p
            dp_buf[t, :, at] = dp
        if 0 in members:
            kv_t[KEY, :, span_at(place)] = key.T
            kv_t[VAL, :, span_at(place)] = value.T

    turn(0)
    q_sib.wait_recv()
    g_sib.wait_recv()
    turn(SIB)
    arrived(REACH)
    hops(REACH, "start")
    arrived(1)
    arrived(2)

    def near_pairs(t, carry):
        forward(t, (0, SIB), t)

        @pl.when(t == 1)
        def _():
            q_pair.wait_recv()
            q_diag.start()

        return carry

    def near_pairs_mate(t, carry):
        forward(t, (PAIR,), t)
        return carry

    def near_pairs_diag(t, carry):
        forward(t, (DIAG,), t)
        return carry

    far = (0, half - 1, half - 2)

    def far_bias():
        for i, t in enumerate(far):
            bias[span_at(i), :] = jnp.where(ahead <= reach_at(t), 0.0, HIDDEN)

    def far_pairs():
        def joined(kind):
            return jnp.concatenate([kv[t, side, kind] for t in far for side in range(2)], axis=0)

        key, value = joined(KEY), joined(VAL)
        for row in range(8):
            at = slice(row * 256, (row + 1) * 256)
            top_at, sum_at, dot_at = [slice(8 * i + row, 8 * i + row + 1) for i in range(3)]
            s = dot(key, q_t[:, at]) * exponent_scale + bias[...]
            top = stat[top_at, :]
            new_top = jnp.maximum(top, jnp.max(s, axis=0, keepdims=True))
            p = jnp.exp2(s - new_top)
            dp = dot(value, g_t[:, at])
            shrink = jnp.exp2(top - new_top)
            stat[sum_at, :] = stat[sum_at, :] * shrink + jnp.sum(p, axis=0, keepdims=True)
            stat[dot_at, :] = stat[dot_at, :] * shrink + jnp.sum(p * dp, axis=0, keepdims=True)
            stat[top_at, :] = new_top
            for i, t in enumerate(far):
                m_blk[t, row : row + 1, :] = new_top
                p_buf[t, :, at] = p[i * SPAN : (i + 1) * SPAN]
                dp_buf[t, :, at] = dp[i * SPAN : (i + 1) * SPAN]

    def far_turn():
        for t in far:
            for kind in (KEY, VAL):
                kv_t[kind, :, span_at(t)] = jnp.concatenate([kv[t, 0, kind], kv[t, 1, kind]], axis=0).T

    lax.fori_loop(1, REACH + 1, near_pairs, 0)

    @pl.when(speaks)
    def _():
        pl.semaphore_wait(word_sem.at[0], 2)
        word(word_sem.at[1], speaker(1))

    g_pair.wait_recv()
    g_diag.start()
    turn(PAIR)
    lax.fori_loop(1, REACH + 1, near_pairs_mate, 0)
    q_diag.wait_recv()
    g_diag.wait_recv()
    turn(DIAG)

    @pl.when(speaks)
    def _():
        pl.semaphore_wait(word_sem.at[1], 1)
        for step in range(1, 4):
            word(word_sem.at[2], lax.rem(column + step, 4) * 16 + place * 4 + member)

    lax.fori_loop(1, REACH + 1, near_pairs_diag, 0)
    far_bias()
    for t in range(REACH + 1, half + 1):
        arrived(t)
    far_pairs()

    for copy in stats:
        copy.start()
    far_turn()
    for copy in stats:
        copy.wait()

    def seen_by(bits, kind):
        if bits == 0:
            return stat[8 * kind : 8 * kind + 8, :]
        order = [8 * kind + 2 * (own ^ bits) for own in range(4)]
        return jnp.concatenate([stat_in[bits - 1, at : at + 2, :] for at in order], axis=0)

    tops = [seen_by(bits, 0) for bits in range(4)]
    top = jnp.maximum(jnp.maximum(tops[0], tops[1]), jnp.maximum(tops[2], tops[3]))
    weights = [jnp.exp2(one - top) for one in tops]
    total = sum(seen_by(bits, 1) * weights[bits] for bits in range(4))
    inverse = 1.0 / total
    both[0] = top
    both[1] = inverse
    both[2] = sum(seen_by(bits, 2) * weights[bits] for bits in range(4)) * inverse

    def grads_of(t):
        factor = jnp.exp2(m_blk[t] - both[0]) * both[1]
        row_dots = both[2]
        part = span_at(t)
        for row in range(8):
            at = slice(row * 256, (row + 1) * 256)
            p = p_buf[t, :, at] * factor[row : row + 1]
            pb[part, at] = p.astype(BF16)
            dsb[part, at] = (p * (dp_buf[t, :, at] - row_dots[row : row + 1])).astype(BF16)
        return dot(dsb[part, :], q8[...]) * score_scale, dot(pb[part, :], g8[...])

    def rows_of(bits):
        at = slice(bits * 512, (bits + 1) * 512)
        return dot(kv_t[VAL], pb[:, at]), dot(kv_t[KEY], dsb[:, at])

    def pass_on(direction, d):
        src, dst = rs_out.at[direction, d - 1], rs_in.at[direction, d - 1]
        if isinstance(d, int) and d == half:
            kind = KEY if direction == PLUS else VAL
            src, dst = src.at[kind], dst.at[kind]
        reach = (d - 1) % REACH + 1
        return remote(src, dst, rs_send.at[direction, d - 1], rs_recv.at[direction, d - 1], along(direction, reach), head)

    def side(direction):
        return slice(PIECE, 2 * PIECE) if direction == PLUS else slice(0, PIECE)

    grads = grads_of(0)
    for direction, kind in ((PLUS, KEY), (MINUS, VAL)):
        rs_out[direction, half - 1, kind] = grads[kind][PIECE:].astype(BF16)
        pass_on(direction, half).start()
    for kind in (KEY, VAL):
        own_grad[kind] = grads[kind][:PIECE]

    def reduce_step(i, carry):
        d = half - 1 - i - i // 2
        grads = grads_of(d)
        for direction in (PLUS, MINUS):
            for kind in (KEY, VAL):
                rs_out[direction, d - 1, kind] = grads[kind][side(direction)].astype(BF16)
            pass_on(direction, d).start()
        return carry

    lax.fori_loop(0, half - 2, reduce_step, 0)

    grads = grads_of(REACH)
    for kind in (KEY, VAL):
        near_grad[kind] = grads[kind]
    for i, bits in enumerate((SIB, DIAG)):
        for j, rows_sum in enumerate(rows_of(bits)):
            mid_out[i, j] = rows_sum.astype(BF16)
    mid.start()
    o_t[1], dq_t[1] = rows_of(PAIR)
    for direction in (PLUS, MINUS):
        for d in range(REACH + 1, half + 1):
            pass_on(direction, d).wait_recv()
        for kind in (KEY, VAL):
            beyond = sum(rs_in[direction, d - 1, kind].astype(F32) for d in range(REACH + 1, half + 1))
            rs_out[direction, REACH - 1, kind] = (near_grad[kind, side(direction), :] + beyond).astype(BF16)
        pass_on(direction, REACH).start()

    mid.wait_recv()
    last_out[0] = (o_t[1] + mid_in[1, 0].astype(F32)).astype(BF16)
    last_out[1] = (dq_t[1] + mid_in[1, 1].astype(F32)).astype(BF16)
    last.start()
    o_t[0], dq_t[0] = rows_of(0)

    @pl.when(jnp.logical_not(speaks))
    def _():
        pl.semaphore_wait(word_sem.at[2], 1)

    for direction in (PLUS, MINUS):
        for d in range(1, REACH + 1):
            pass_on(direction, d).wait_recv()
    for kind in (KEY, VAL):
        total = own_grad[kind]
        for direction in (PLUS, MINUS):
            for d in range(1, REACH + 1):
                total += rs_in[direction, d - 1, kind].astype(F32)
        for n in range(QUADS):
            f_out[n, 4 * kind : 4 * kind + 4, :] = total[4 * n : 4 * n + 4]

    def to_owner(n):
        return remote(f_out.at[n], f_in.at[quad], f_send.at[n], f_recv.at[0], z, member * 16 + n)

    row_of_chips = lax.rem(head, 16) // 2
    places = [(away, other) for away in (4, 3, 5, 2, 6, 1, 7, 0) for other in range(2)]

    def owner(away, other):
        return 2 * lax.rem(row_of_chips + away, 8) + other

    for away, other in places:
        n = owner(away, other)
        if away:
            to_owner(n).start()
        else:
            here = head == member * 16 + n

            @pl.when(here)
            def _():
                pltpu.make_async_copy(f_out.at[n], f_in.at[quad], f_recv.at[0]).start()

            @pl.when(jnp.logical_not(here))
            def _():
                to_owner(n).start()

    last.wait_recv()
    for h in range(2):
        at = slice(h * 256, (h + 1) * 256)
        cols_h = slice(h * HEAD_DIM, (h + 1) * HEAD_DIM)
        for i, part, out, scale in ((0, o_t, rows_ref.at[0], 1.0), (1, dq_t, rows_ref.at[1], score_scale)):
            rows_sum = part[0, :, at] + mid_in[0, i, :, at].astype(F32) + last_in[i, :, at].astype(F32)
            out[:, cols_h] = (rows_sum * scale).T.astype(BF16)

    for copy in (q_sib, g_sib, q_pair, g_pair, q_diag, g_diag, mid, last):
        copy.wait_send()
    for source in range(0, half, REACH):
        hops(source, "wait_send")
    for direction in (PLUS, MINUS):
        for d in range(1, half + 1):
            pass_on(direction, d).wait_send()
    for away, other in places:
        n = owner(away, other)
        if away:
            to_owner(n).wait_send()
        else:

            @pl.when(head != member * 16 + n)
            def _():
                to_owner(n).wait_send()

    pltpu.make_async_copy(f_out, f_in, f_recv.at[0]).wait()
    for g in range(QUADS // 2):
        at = slice(g * HEAD_DIM, (g + 1) * HEAD_DIM)
        summed = f_in[2 * g] + f_in[2 * g + 1]
        grads_ref[:, at] = summed.astype(BF16)


def per_device(query_rows, key_rows, value_rows, out_grad, span_order):
    n_ctx = lax.axis_size("ctx")
    half = n_ctx // 2
    vmem = pltpu.VMEM
    dma = pltpu.SemaphoreType.DMA
    outside = pl.BlockSpec(memory_space=pltpu.HBM)
    local = pl.BlockSpec(memory_space=pltpu.VMEM)
    rows, grads = pl.pallas_call(
        functools.partial(attention_kernel, n_ctx),
        out_shape=(
            jax.ShapeDtypeStruct((2, 256, 256), BF16),
            jax.ShapeDtypeStruct((8, 1024), BF16),
        ),
        in_specs=[pl.BlockSpec(memory_space=pltpu.SMEM), outside, outside, outside, outside],
        out_specs=(local, local),
        scratch_shapes=[
            vmem((2048, 128), BF16),
            vmem((2048, 128), BF16),
            vmem((128, 2048), BF16),
            vmem((128, 2048), BF16),
            vmem((3 * SPAN, 256), F32),
            vmem((half, 2, 2, PIECE, 128), BF16),
            vmem((2, 128, half * 128), BF16),
            vmem((half, 128, 2048), F32),
            vmem((half, 128, 2048), F32),
            vmem((half, 8, 256), F32),
            vmem((24, 256), F32),
            vmem((3, 24, 256), F32),
            vmem((3, 8, 256), F32),
            vmem((half * 128, 2048), BF16),
            vmem((half * 128, 2048), BF16),
            vmem((2, 128, 512), F32),
            vmem((2, 128, 512), F32),
            vmem((2, 2, 128, 512), BF16),
            vmem((2, 2, 128, 512), BF16),
            vmem((2, 128, 512), BF16),
            vmem((2, 128, 512), BF16),
            vmem((2, PIECE, 128), F32),
            vmem((2, 2 * PIECE, 128), F32),
            vmem((2, half, 2, PIECE, 128), BF16),
            vmem((2, half, 2, PIECE, 128), BF16),
            vmem((QUADS, 8, 128), F32),
            vmem((QUADS, 8, 128), F32),
            dma((6,)),
            dma((11,)),
            dma((11,)),
            dma((2, half)),
            dma((2, half)),
            dma((2, half)),
            dma((2, half)),
            dma((QUADS,)),
            dma((1,)),
            pltpu.SemaphoreType.REGULAR((3,)),
        ],
        compiler_params=pltpu.CompilerParams(
            collective_id=0, has_side_effects=True, vmem_limit_bytes=62 * 1024 * 1024
        ),
    )(span_order, query_rows, key_rows, value_rows, out_grad)
    return rows[0], rows[1], grads[:4], grads[4:]


def solution(mesh):
    in_specs = (P("ctx", "head"), P("ctx", None), P("ctx", None), P("ctx", "head"), P())
    out_specs = (
        P("ctx", "head"),
        P("ctx", "head"),
        P(("ctx", "head"), None),
        P(("ctx", "head"), None),
    )
    return jax.shard_map(
        per_device, mesh=mesh, in_specs=in_specs, out_specs=out_specs, check_vma=False
    )
```
